32 devices in a mesh: groups: 2 (over y), span: 4 (over z), head: 4 (over x, core).
Axes of the slice: x: 2, y: 2, z: 4, core: 2. Of those that a mesh axis runs over, the one named last changes fastest.
Arguments:
- query_rows: bfloat16 [2048, 6144], P(('groups', 'span', 'head')), parts along dimension 0, may hold values from -6 to 6
- key_rows: bfloat16 [2048, 1024], P(('groups', 'span', 'head')), parts along dimension 0, may hold values from -6 to 6
- value_rows: bfloat16 [2048, 1024], P(('groups', 'span', 'head')), parts along dimension 0, may hold values from -6 to 6
- frame_counts: int32 [16], P('groups'), parts along dimension 0, may hold values from 1 to 4, as said below
- noise_levels: int32 [16], P('groups'), parts along dimension 0, may hold values from 0 to 63
- span_mask: int32 [16, 8], P('groups'), parts along dimension 0, may hold values from 0 to 1, as said below
- level_gate: bfloat16 [64, 6144], P(None, 'head'), may hold values from 0.19921875 to 1.796875
Outputs:
- attended: bfloat16 [2048, 6144], P(('groups', 'span', 'head')), parts along dimension 0
The draws below stay inside these ranges and needn't reach their ends.
There are 2 independent parts, one for each index of `groups`. The reference program is written for one: setup_inputs(seed, part) draws one part's arguments, and reference() takes and returns one part's arrays. A program takes and returns all parts, laid end to end along the dimension named above; an argument that names none is the same for every part. Nothing has to cross between parts.
Inputs may be any that keep to these rules, and one draw needn't show every extreme that they name: `frame_counts`: each span holds at least one frame, and some span holds exactly 4. span_mask[c, c] = 1 for every span, span_mask[c, e] = 0 for e > c, entries below the diagonal are 0 or 1.
All inputs are finite; a program needn't handle non-finite values.
Results may differ from the reference program's by a relative error of at most 0.0033.
Values may be sent and summed in bfloat16 or wider, within the bound.
A program may use at most 64 MiB of HBM per device.

```python
import math
import jax
import jax.numpy as jnp
from jax import lax

HEADS = 48
KV_HEADS = 8
HD = 128
D = 6144
FRAME_TOK = 32
FMAX = 4
CT = 128
SPANS = 8
ROWS = 1024
LEVELS = 64


def draw_query_rows(key, part):
    return jnp.clip(1.7 * jax.random.normal(jax.random.fold_in(key, 5), (ROWS, D), jnp.float32), -6.0, 6.0).astype(jnp.bfloat16)


def draw_key_rows(key, part):
    return jnp.clip(1.7 * jax.random.normal(jax.random.fold_in(key, 6), (ROWS, KV_HEADS * HD), jnp.float32), -6.0, 6.0).astype(jnp.bfloat16)


def draw_frame_counts(key, part):
    frame_draw = jax.random.randint(jax.random.fold_in(key, 11), (SPANS,), 1, FMAX + 1, jnp.int32)
    busiest = jax.random.randint(jax.random.fold_in(key, 12), (), 0, SPANS, jnp.int32)
    return jnp.where(jnp.arange(SPANS, dtype=jnp.int32) == busiest, jnp.int32(FMAX), frame_draw).astype(jnp.int32)


def draw_span_mask(key, part):
    coin_flip = jax.random.randint(jax.random.fold_in(key, 13), (SPANS, SPANS), 0, 4, jnp.int32)
    row_index = jnp.arange(SPANS, dtype=jnp.int32)[:, None]
    col_index = jnp.arange(SPANS, dtype=jnp.int32)[None, :]
    below = jnp.where(col_index < row_index, (coin_flip > 0).astype(jnp.int32), 0)
    return jnp.where(col_index == row_index, 1, below).astype(jnp.int32)


def set_ends(array, stream_key, smallest, top_value):
    shape = array.shape
    index_at = [jax.random.randint(jax.random.fold_in(stream_key, axis), (), 0, shape[axis]) for axis in range(len(shape))]
    array = array.at[tuple(index_at)].set(smallest)
    longest = shape.index(max(shape))
    index_at[longest] = (index_at[longest] + 1) % shape[longest]
    return array.at[tuple(index_at)].set(top_value)


def block_levels(rng, shape, cuts, least, top_value):
    def one(dim, shards_of):
        heights = jax.random.uniform(jax.random.fold_in(jax.random.fold_in(rng, 6), dim), (shards_of,), jnp.float32, least / len(cuts), top_value / len(cuts))
        return jnp.repeat(jnp.exp(heights), shape[dim] // shards_of).reshape((-1,) + (1,) * (len(shape) - dim - 1))

    gain = one(*cuts[0])
    for cut in cuts[1:]:
        gain = gain * one(*cut)
    return gain


def scatter_about(rng, extent, scale, most, shards=(), held_as=jnp.bfloat16):
    level = block_levels(rng, extent, shards, -0.22, 0.18) if shards else 1.0
    values = jax.random.normal(rng, extent, jnp.float32) * scale * level
    return jnp.minimum(jnp.maximum(values, -most), most).astype(held_as)


def setup_inputs(seed: int = 0, part: int = 0) -> dict:
    key_of = jax.random.split(jax.random.key(seed), 8)
    part_keys = jax.random.split(jax.random.fold_in(key_of[7], part), 8)
    return {
        "query_rows": draw_query_rows(jax.random.fold_in(jax.random.fold_in(key_of[7], part), 71), part),
        "key_rows": draw_key_rows(jax.random.fold_in(jax.random.fold_in(key_of[7], part), 71), part),
        "value_rows": scatter_about(part_keys[2], (ROWS, KV_HEADS * HD), 1.0, 6.0, ((0, 16),)),
        "frame_counts": draw_frame_counts(jax.random.fold_in(jax.random.fold_in(key_of[7], part), 71), part),
        "noise_levels": set_ends(jax.random.randint(part_keys[4], (SPANS,), 0, LEVELS), jax.random.fold_in(part_keys[4], 1), 0, LEVELS - 1).astype(jnp.int32),
        "span_mask": draw_span_mask(jax.random.fold_in(jax.random.fold_in(key_of[7], part), 71), part),
        "level_gate": jnp.clip(0.19921875 + 1.5976562 * jax.random.uniform(key_of[6], (LEVELS, D), jnp.float32) ** block_levels(key_of[6], (LEVELS, D), ((1, 4),), -0.2, 0.2), 0.19921875, 1.796875).astype(jnp.bfloat16),
    }


def reference(query_rows, key_rows, value_rows, frame_counts, noise_levels, span_mask, level_gate):
    total_rows = query_rows.shape[0]
    span_count = total_rows // CT
    group_size = HEADS // KV_HEADS
    score_scale = 1.0 / math.sqrt(HD)
    position = jnp.arange(CT, dtype=jnp.int32)
    live_rows = position[None, :] < (frame_counts * FRAME_TOK)[:, None]
    live_flat = live_rows.reshape(-1)
    key_heads = key_rows.reshape(total_rows, KV_HEADS, HD).astype(jnp.float32)
    value_heads = value_rows.reshape(total_rows, KV_HEADS, HD).astype(jnp.float32)

    def one_span(span_index):
        mask_row = lax.dynamic_index_in_dim(span_mask, span_index, 0, keepdims=False)
        usable = (jnp.repeat(mask_row, CT, total_repeat_length=total_rows) > 0) & live_flat
        queries = lax.dynamic_slice_in_dim(query_rows, span_index * CT, CT, 0)
        queries = queries.reshape(CT, KV_HEADS, group_size, HD).astype(jnp.float32)

        def one_head(head_index):
            query_head = lax.dynamic_index_in_dim(queries, head_index, 1, keepdims=False)
            key_head = lax.dynamic_index_in_dim(key_heads, head_index, 1, keepdims=False)
            value_head = lax.dynamic_index_in_dim(value_heads, head_index, 1, keepdims=False)
            scores = jnp.einsum('qgd,kd->gqk', query_head, key_head) * score_scale
            masked = jnp.where(usable[None, None, :], scores, -jnp.inf)
            row_max = lax.optimization_barrier(jnp.max(masked, axis=2, keepdims=True))
            exponent = jnp.exp(masked - row_max)
            denominator = lax.optimization_barrier(jnp.sum(exponent, axis=2))
            weights = lax.optimization_barrier(exponent.astype(jnp.bfloat16)).astype(jnp.float32)
            numerator = jnp.einsum('gqk,kd->qgd', weights, value_head)
            return numerator / jnp.transpose(denominator)[:, :, None]
        outputs = lax.map(one_head, jnp.arange(KV_HEADS, dtype=jnp.int32))
        outputs = jnp.transpose(outputs, (1, 0, 2, 3)).reshape(CT, KV_HEADS * group_size * HD)
        level_index = lax.dynamic_index_in_dim(noise_levels, span_index, 0, keepdims=False)
        gate_row = lax.dynamic_index_in_dim(level_gate, level_index, 0, keepdims=False).astype(jnp.float32)
        query_live = lax.dynamic_index_in_dim(live_rows, span_index, 0, keepdims=False)
        result = jnp.where(query_live[:, None], outputs * gate_row[None, :], jnp.float32(0.0))
        return result.astype(jnp.bfloat16)
    blocks = lax.map(one_span, jnp.arange(span_count, dtype=jnp.int32))
    return blocks.reshape(total_rows, KV_HEADS * group_size * HD)
```

```python
import functools
import math

import jax
import jax.numpy as jnp
from jax import lax
from jax.experimental import pallas as pl
from jax.experimental.pallas import tpu as pltpu
from jax.sharding import PartitionSpec as P

HD = 128
FRAME_TOK = 32
CT = 128
CORES = 2
MESH = pl.DeviceIdType.MESH
LOW = -1e30


def kernel(
    levels, peers,
    q_ref, k_ref, v_ref, frames_ref, noise_ref, mask_ref, gate_ref,
    out_ref,
    kbuf, vbuf, acc, top, gate_out, gate_in,
    recv_sem, up_sem, across_sem, sib_sem, gate_send, gate_recv,
):
    rows = q_ref.shape[0]
    kv_heads = k_ref.shape[1] // HD
    heads = q_ref.shape[1] // HD
    group = heads // kv_heads
    heads_dev = gate_ref.shape[1] // HD
    chips = peers // CORES
    level_rows = peers * rows
    level_spans = level_rows // CT
    factor = math.log2(math.e) / math.sqrt(HD)

    z = lax.axis_index("span")
    me = lax.axis_index("head")
    chip, core = me // CORES, me % CORES
    sibling = chip * CORES + (1 - core)
    bufs = (kbuf, vbuf)

    barrier = pltpu.get_barrier_semaphore()
    for step in range(1, peers):
        pl.semaphore_signal(
            barrier, inc=1, device_id={"head": (me + step) % peers}, device_id_type=MESH
        )

    @pl.when(z > 0)
    def _():
        pl.semaphore_signal(barrier, inc=1, device_id={"span": z - 1}, device_id_type=MESH)

    kbuf[z, me] = k_ref[...]
    vbuf[z, me] = v_ref[...]
    acc[...] = jnp.zeros_like(acc)
    top[...] = jnp.full_like(top, LOW)
    for i in range(level_spans):
        level_index = noise_ref[z * level_spans + i]
        pick = lax.broadcasted_iota(jnp.int32, (8, gate_ref.shape[0]), 1) == level_index
        picked = jnp.dot(
            pick.astype(jnp.bfloat16), gate_ref[...], preferred_element_type=jnp.float32
        )
        for n in range(heads_dev):
            gate_out[i, n : n + 1, :] = picked[0:1, n * HD : (n + 1) * HD]

    pl.semaphore_wait(barrier, peers - 1 + jnp.where(z < levels - 1, 1, 0))

    def copy(kv, level, slot, send_sem, target):
        return pltpu.make_async_remote_copy(
            src_ref=bufs[kv].at[level, slot],
            dst_ref=bufs[kv].at[level, slot],
            send_sem=send_sem,
            recv_sem=recv_sem.at[level, slot, kv],
            device_id=target,
            device_id_type=MESH,
        )

    def up(kv, level):
        return copy(kv, level, me, up_sem.at[level, kv], {"span": z + 1})

    def across(kv, level, step):
        other = (chip + step) % chips
        return copy(
            kv, level, me, across_sem.at[level, step - 1, kv], {"head": other * CORES + core}
        )

    def to_sibling(kv, level, step):
        slot = ((chip + step) % chips) * CORES + core
        return copy(kv, level, slot, sib_sem.at[level, step, kv], {"head": sibling})

    def wait_slot(kv, level, slot):
        copy(kv, level, slot, up_sem.at[level, kv], {"head": sibling}).wait_recv()

    def issue(kv, level):
        @pl.when(z < levels - 1)
        def _():
            up(kv, level).start()

        for step in range(1, chips):
            across(kv, level, step).start()
        to_sibling(kv, level, 0).start()

    def gate_copy(step):
        target = (me + step) % peers
        return pltpu.make_async_remote_copy(
            src_ref=gate_out.at[(target * rows) // CT],
            dst_ref=gate_in.at[me],
            send_sem=gate_send.at[step],
            recv_sem=gate_recv.at[me],
            device_id={"head": target},
            device_id_type=MESH,
        )

    for kv in range(2):
        issue(kv, z)
    for step in range(1, peers):
        gate_copy(step).start()

    token = me * rows
    span = z * level_spans + token // CT
    gate_in[me] = gate_out[token // CT]

    def fold(level):
        column = lax.broadcasted_iota(jnp.int32, (1, level_rows), 1)
        usable = column < 0
        for i in range(level_spans):
            key_span = level * level_spans + i
            limit = jnp.where(mask_ref[span, key_span] > 0, frames_ref[key_span] * FRAME_TOK, 0)
            usable = usable | ((column >= i * CT) & (column < i * CT + limit))
        bias = jnp.where(usable, jnp.float32(0.0), jnp.float32(LOW))
        ones = jnp.ones((level_rows, HD), jnp.bfloat16)

        def one_head(j, carry):
            lanes = pl.ds(pl.multiple_of(j * HD, HD), HD)
            queries = jnp.concatenate(
                [
                    q_ref[:, pl.ds(pl.multiple_of((j * group + g) * HD, HD), HD)]
                    for g in range(group)
                ],
                axis=0,
            )
            keys = kbuf[level, :, :, lanes].reshape(level_rows, HD)
            values = vbuf[level, :, :, lanes].reshape(level_rows, HD)
            scores = lax.dot_general(
                queries, keys, (((1,), (1,)), ((), ())), preferred_element_type=jnp.float32
            )
            scores = scores + bias
            old = top[j]
            new = jnp.maximum(old, jnp.max(scores, axis=1, keepdims=True))
            top[j] = new
            weights = jnp.exp2((scores - new[:, :1]) * factor).astype(jnp.bfloat16)
            update = jnp.dot(
                weights,
                jnp.concatenate([values, ones], axis=1),
                preferred_element_type=jnp.float32,
            )
            shrink = jnp.exp2((old - new) * factor)
            acc[j] = acc[j] * jnp.concatenate([shrink, shrink], axis=1) + update
            return carry

        lax.fori_loop(0, kv_heads, one_head, 0)

    def one_level(s, carry):
        level = z - s

        @pl.when(s < z)
        def _():
            for kv in range(2):
                wait_slot(kv, level - 1, me)
                issue(kv, level - 1)

        for kv in range(2):
            for step in range(1, chips):
                wait_slot(kv, level, ((chip + step) % chips) * CORES + core)
                to_sibling(kv, level, step).start()
        for kv in range(2):
            for step in range(chips):
                wait_slot(kv, level, ((chip + step) % chips) * CORES + 1 - core)
        fold(level)
        return carry

    lax.fori_loop(0, z + 1, one_level, 0)

    for step in range(1, peers):
        source = (me + step) % peers
        pltpu.make_async_remote_copy(
            src_ref=gate_out.at[0],
            dst_ref=gate_in.at[source],
            send_sem=gate_send.at[step],
            recv_sem=gate_recv.at[source],
            device_id={"head": source},
            device_id_type=MESH,
        ).wait_recv()

    position = token % CT + lax.broadcasted_iota(jnp.int32, (rows, HD), 0)
    live = position < frames_ref[span] * FRAME_TOK

    def finish(j, carry):
        for g in range(group):
            head = j * group + g
            part = slice(g * rows, (g + 1) * rows)
            gate = gate_in[head // heads_dev, pl.ds(head % heads_dev, 1), :]
            ratio = acc[j, part, :HD] / acc[j, part, HD:]
            out_ref[:, pl.ds(pl.multiple_of(head * HD, HD), HD)] = jnp.where(
                live, ratio * gate, jnp.float32(0.0)
            ).astype(out_ref.dtype)
        return carry

    lax.fori_loop(0, kv_heads, finish, 0)

    def drain(s, carry):
        level = z - s
        for kv in range(2):
            @pl.when(z < levels - 1)
            def _():
                up(kv, level).wait_send()

            for step in range(1, chips):
                across(kv, level, step).wait_send()
            for step in range(chips):
                to_sibling(kv, level, step).wait_send()
        return carry

    lax.fori_loop(0, z + 1, drain, 0)
    for step in range(1, peers):
        gate_copy(step).wait_send()


def body(levels, peers, q, k, v, frames, noise, mask, gate):
    rows, kv_width = k.shape
    kv_heads = kv_width // HD
    group_rows = q.shape[1] // kv_width * rows
    chips = peers // CORES
    level_spans = peers * rows // CT
    gate_rows = -(-(gate.shape[1] // HD) // 8) * 8
    vmem = pl.BlockSpec(memory_space=pltpu.VMEM)
    smem = pl.BlockSpec(memory_space=pltpu.SMEM)
    pairs = q.shape[0] * q.shape[1] // HD * levels * peers * rows
    return pl.pallas_call(
        functools.partial(kernel, levels, peers),
        out_shape=jax.ShapeDtypeStruct(q.shape, q.dtype),
        in_specs=[vmem, vmem, vmem, smem, smem, smem, vmem],
        out_specs=vmem,
        scratch_shapes=[
            pltpu.VMEM((levels, peers, rows, kv_width), k.dtype),
            pltpu.VMEM((levels, peers, rows, kv_width), v.dtype),
            pltpu.VMEM((kv_heads, group_rows, 2 * HD), jnp.float32),
            pltpu.VMEM((kv_heads, group_rows, HD), jnp.float32),
            pltpu.VMEM((level_spans, gate_rows, HD), jnp.float32),
            pltpu.VMEM((peers, gate_rows, HD), jnp.float32),
            pltpu.SemaphoreType.DMA((levels, peers, 2)),
            pltpu.SemaphoreType.DMA((levels, 2)),
            pltpu.SemaphoreType.DMA((levels, max(chips - 1, 1), 2)),
            pltpu.SemaphoreType.DMA((levels, chips, 2)),
            pltpu.SemaphoreType.DMA((peers,)),
            pltpu.SemaphoreType.DMA((peers,)),
        ],
        compiler_params=pltpu.CompilerParams(
            collective_id=0, has_side_effects=True, vmem_limit_bytes=40 << 20
        ),
        cost_estimate=pl.CostEstimate(
            flops=pairs * HD * 4, bytes_accessed=4 * q.size, transcendentals=pairs
        ),
    )(q, k, v, frames, noise, mask, gate)


def solution(mesh):
    placed = (
        P(("groups", "span", "head"), None),
        P(("groups", "span", "head"), None),
        P(("groups", "span", "head"), None),
        P("groups"),
        P("groups"),
        P("groups", None),
        P(None, "head"),
    )
    return jax.shard_map(
        functools.partial(body, mesh.shape["span"], mesh.shape["head"]),
        mesh=mesh,
        in_specs=placed,
        out_specs=P(("groups", "span", "head"), None),
        check_vma=False,
    )
```

```python
import functools
import math

import jax
import jax.numpy as jnp
from jax import lax
from jax.experimental import pallas as pl
from jax.experimental.pallas import tpu as pltpu
from jax.sharding import PartitionSpec as P

HD = 128
FRAME_TOK = 32
CT = 128
CORES = 2
MESH = pl.DeviceIdType.MESH
LOW = -1e30


def kernel(
    levels, peers, units,
    q_hbm, k_hbm, v_hbm, frames_hbm, noise_hbm, mask_hbm, gate_hbm,
    out_ref,
    kv_buf, q_ref, gate_ref, frames_ref, noise_ref, mask_ref, acc, top, gate_out, gate_in,
    recv_sem, up_sem, across_sem, sib_sem, gate_send, gate_recv, own_sem, load_sem,
):
    rows, kv_width = k_hbm.shape
    kv_heads = kv_width // HD
    heads = q_hbm.shape[1] // HD
    group = heads // kv_heads
    heads_dev = gate_hbm.shape[1] // HD
    chips = peers // CORES
    level_rows = peers * rows
    level_spans = level_rows // CT
    unit_heads = kv_heads // units
    unit_width = unit_heads * HD
    factor = math.log2(math.e) / math.sqrt(HD)

    z = lax.axis_index("span")
    me = lax.axis_index("head")
    chip, core = me // CORES, me % CORES
    sibling = chip * CORES + (1 - core)

    barrier = pltpu.get_barrier_semaphore()
    for step in range(1, peers):
        pl.semaphore_signal(
            barrier, inc=1, device_id={"head": (me + step) % peers}, device_id_type=MESH
        )

    @pl.when(z > 0)
    def _():
        pl.semaphore_signal(barrier, inc=1, device_id={"span": z - 1}, device_id_type=MESH)

    def piece(kv, unit):
        return (k_hbm, v_hbm)[kv].at[:, pl.ds(unit * unit_width, unit_width)]

    loads = [
        pltpu.make_async_copy(source, target, load_sem.at[n])
        for n, (source, target) in enumerate(
            (
                (frames_hbm, frames_ref),
                (noise_hbm, noise_ref),
                (mask_hbm, mask_ref),
                (gate_hbm, gate_ref),
                (q_hbm, q_ref),
            )
        )
    ]
    for load in loads:
        load.start()
    own = [
        [
            pltpu.make_async_copy(piece(kv, u), kv_buf.at[z, u, me, kv], own_sem.at[u, kv])
            for kv in range(2)
        ]
        for u in range(units)
    ]
    for u in range(units):
        for kv in range(2):
            own[u][kv].start()

    pl.semaphore_wait(barrier, peers - 1 + jnp.where(z < levels - 1, 1, 0))

    def copy(level, unit, slot, send_sem, target, kv=None):
        place = kv_buf.at[level, unit, slot]
        return pltpu.make_async_remote_copy(
            src_ref=place if kv is None else piece(kv, unit),
            dst_ref=place if kv is None else place.at[kv],
            send_sem=send_sem,
            recv_sem=recv_sem.at[level, unit, slot],
            device_id=target,
            device_id_type=MESH,
        )

    def up(level, unit, kv=None):
        return copy(level, unit, me, up_sem.at[level, unit], {"span": z + 1}, kv)

    def across(level, unit, step, kv=None):
        other = (chip + step) % chips
        return copy(
            level, unit, me, across_sem.at[level, unit, step - 1],
            {"head": other * CORES + core}, kv,
        )

    def to_sibling(level, unit, step, kv=None):
        slot = ((chip + step) % chips) * CORES + core
        return copy(level, unit, slot, sib_sem.at[level, unit, step], {"head": sibling}, kv)

    def wait_slot(level, unit, slot):
        copy(level, unit, slot, up_sem.at[level, unit], {"head": sibling}).wait_recv()

    def issue(level, unit, kv=None):
        @pl.when(z < levels - 1)
        def _():
            up(level, unit, kv).start()

        for step in range(1, chips):
            across(level, unit, step, kv).start()
        to_sibling(level, unit, 0, kv).start()

    def gate_copy(step):
        target = (me + step) % peers
        return pltpu.make_async_remote_copy(
            src_ref=gate_out.at[(target * rows) // CT],
            dst_ref=gate_in.at[me],
            send_sem=gate_send.at[step],
            recv_sem=gate_recv.at[me],
            device_id={"head": target},
            device_id_type=MESH,
        )

    for u in range(units):
        for kv in range(2):
            issue(z, u, kv)

    acc[...] = jnp.zeros_like(acc)
    top[...] = jnp.full_like(top, LOW)
    for load in loads:
        load.wait()
    for i in range(level_spans):
        level_index = noise_ref[z * level_spans + i]
        pick = lax.broadcasted_iota(jnp.int32, (8, gate_ref.shape[0]), 1) == level_index
        picked = jnp.dot(
            pick.astype(jnp.bfloat16), gate_ref[...], preferred_element_type=jnp.float32
        )
        for n in range(heads_dev):
            gate_out[i, n : n + 1, :] = picked[0:1, n * HD : (n + 1) * HD]
    for step in range(1, peers):
        gate_copy(step).start()

    token = me * rows
    span = z * level_spans + token // CT
    gate_in[me] = gate_out[token // CT]
    for u in range(units):
        for kv in range(2):
            own[u][kv].wait()

    def fold(level, unit):
        column = lax.broadcasted_iota(jnp.int32, (1, level_rows), 1)
        usable = column < 0
        for i in range(level_spans):
            key_span = level * level_spans + i
            limit = jnp.where(mask_ref[span, key_span] > 0, frames_ref[key_span] * FRAME_TOK, 0)
            usable = usable | ((column >= i * CT) & (column < i * CT + limit))
        bias = jnp.where(usable, jnp.float32(0.0), jnp.float32(LOW))
        ones = jnp.ones((level_rows, HD), jnp.bfloat16)

        for n in range(unit_heads):
            j = unit * unit_heads + n
            lanes = slice(n * HD, (n + 1) * HD)
            queries = jnp.concatenate(
                [
                    q_ref[:, (j * group + g) * HD : (j * group + g + 1) * HD]
                    for g in range(group)
                ],
                axis=0,
            )
            keys = kv_buf[level, unit, :, 0, :, lanes].reshape(level_rows, HD)
            values = kv_buf[level, unit, :, 1, :, lanes].reshape(level_rows, HD)
            scores = lax.dot_general(
                queries, keys, (((1,), (1,)), ((), ())), preferred_element_type=jnp.float32
            )
            scores = scores + bias
            old = top[j]
            new = jnp.maximum(old, jnp.max(scores, axis=1, keepdims=True))
            top[j] = new
            weights = jnp.exp2((scores - new[:, :1]) * factor).astype(jnp.bfloat16)
            update = jnp.dot(
                weights,
                jnp.concatenate([values, ones], axis=1),
                preferred_element_type=jnp.float32,
            )
            shrink = jnp.exp2((old - new) * factor)
            acc[j] = acc[j] * jnp.concatenate([shrink, shrink], axis=1) + update

    def forward(level, unit):
        for step in range(1, chips):
            wait_slot(level, unit, ((chip + step) % chips) * CORES + core)
            to_sibling(level, unit, step).start()

    forward(z, 0)

    def one_level(s, carry):
        level = z - s
        for u in range(units):
            ahead, ahead_unit = (u + 2) // units, (u + 2) % units

            @pl.when((s >= 1) if ahead == 0 else (s + ahead <= z))
            def _():
                wait_slot(level - ahead, ahead_unit, me)
                issue(level - ahead, ahead_unit)

            if u + 1 < units:
                forward(level, u + 1)
            else:
                @pl.when(s < z)
                def _():
                    forward(level - 1, 0)

            for step in range(chips):
                wait_slot(level, u, ((chip + step) % chips) * CORES + 1 - core)
            fold(level, u)
        return carry

    lax.fori_loop(0, z + 1, one_level, 0)

    for step in range(1, peers):
        source = (me + step) % peers
        pltpu.make_async_remote_copy(
            src_ref=gate_out.at[0],
            dst_ref=gate_in.at[source],
            send_sem=gate_send.at[step],
            recv_sem=gate_recv.at[source],
            device_id={"head": source},
            device_id_type=MESH,
        ).wait_recv()

    position = token % CT + lax.broadcasted_iota(jnp.int32, (rows, HD), 0)
    live = position < frames_ref[span] * FRAME_TOK

    for head in range(heads):
        j, g = head // group, head % group
        part = slice(g * rows, (g + 1) * rows)
        row = head % heads_dev
        gate = gate_in[head // heads_dev, row : row + 1, :]
        ratio = acc[j, part, :HD] / acc[j, part, HD:]
        out_ref[:, head * HD : (head + 1) * HD] = jnp.where(
            live, ratio * gate, jnp.float32(0.0)
        ).astype(out_ref.dtype)

    def drain(s, carry):
        level = z - s
        for u in range(units):
            @pl.when(z < levels - 1)
            def _():
                up(level, u).wait_send()

            for step in range(1, chips):
                across(level, u, step).wait_send()
            for step in range(chips):
                to_sibling(level, u, step).wait_send()
        return carry

    lax.fori_loop(0, z + 1, drain, 0)
    for step in range(1, peers):
        gate_copy(step).wait_send()


def body(levels, peers, q, k, v, frames, noise, mask, gate):
    rows, kv_width = k.shape
    kv_heads = kv_width // HD
    group_rows = q.shape[1] // kv_width * rows
    chips = peers // CORES
    units = kv_heads // 2
    level_spans = peers * rows // CT
    gate_rows = -(-(gate.shape[1] // HD) // 8) * 8
    hbm = pl.BlockSpec(memory_space=pltpu.HBM)
    pairs = q.shape[0] * q.shape[1] // HD * levels * peers * rows
    return pl.pallas_call(
        functools.partial(kernel, levels, peers, units),
        out_shape=jax.ShapeDtypeStruct(q.shape, q.dtype),
        in_specs=[hbm] * 7,
        out_specs=pl.BlockSpec(memory_space=pltpu.VMEM),
        scratch_shapes=[
            pltpu.VMEM((levels, units, peers, 2, rows, kv_width // units), k.dtype),
            pltpu.VMEM(q.shape, q.dtype),
            pltpu.VMEM(gate.shape, gate.dtype),
            pltpu.SMEM(frames.shape, frames.dtype),
            pltpu.SMEM(noise.shape, noise.dtype),
            pltpu.SMEM(mask.shape, mask.dtype),
            pltpu.VMEM((kv_heads, group_rows, 2 * HD), jnp.float32),
            pltpu.VMEM((kv_heads, group_rows, HD), jnp.float32),
            pltpu.VMEM((level_spans, gate_rows, HD), jnp.float32),
            pltpu.VMEM((peers, gate_rows, HD), jnp.float32),
            pltpu.SemaphoreType.DMA((levels, units, peers)),
            pltpu.SemaphoreType.DMA((levels, units)),
            pltpu.SemaphoreType.DMA((levels, units, max(chips - 1, 1))),
            pltpu.SemaphoreType.DMA((levels, units, chips)),
            pltpu.SemaphoreType.DMA((peers,)),
            pltpu.SemaphoreType.DMA((peers,)),
            pltpu.SemaphoreType.DMA((units, 2)),
            pltpu.SemaphoreType.DMA((5,)),
        ],
        compiler_params=pltpu.CompilerParams(
            collective_id=0, has_side_effects=True, vmem_limit_bytes=64 << 20
        ),
        cost_estimate=pl.CostEstimate(
            flops=pairs * HD * 4, bytes_accessed=4 * q.size, transcendentals=pairs
        ),
    )(q, k, v, frames, noise, mask, gate)


def solution(mesh):
    placed = (
        P(("groups", "span", "head"), None),
        P(("groups", "span", "head"), None),
        P(("groups", "span", "head"), None),
        P("groups"),
        P("groups"),
        P("groups", None),
        P(None, "head"),
    )
    return jax.shard_map(
        functools.partial(body, mesh.shape["span"], mesh.shape["head"]),
        mesh=mesh,
        in_specs=placed,
        out_specs=P(("groups", "span", "head"), None),
        check_vma=False,
    )
```

```python
import functools
import math

import jax
import jax.numpy as jnp
from jax import lax
from jax.experimental import pallas as pl
from jax.experimental.pallas import tpu as pltpu
from jax.sharding import PartitionSpec as P

HD = 128
FRAME_TOK = 32
CT = 128
CORES = 2
MESH = pl.DeviceIdType.MESH
LOW = -1e30


def kernel(
    levels, peers, units,
    q_hbm, k_hbm, v_hbm, frames_hbm, noise_hbm, mask_hbm, gate_hbm,
    out_hbm,
    kv_buf, q_ref, stage, gate_ref, frames_ref, noise_ref, mask_ref, acc, top, gate_out, gate_in,
    recv_sem, first_sem, up_sem, across_sem, gate_send, gate_recv, own_sem, load_sem,
    q_send, q_recv, out_send, out_recv, out_sem,
):
    rows, kv_width = k_hbm.shape
    kv_heads = kv_width // HD // CORES
    heads = q_hbm.shape[1] // HD // CORES
    group = heads // kv_heads
    heads_dev = gate_hbm.shape[1] // HD
    chips = peers // CORES
    chip_rows = CORES * rows
    level_rows = peers * rows
    level_spans = level_rows // CT
    unit_heads = kv_heads // units
    unit_width = unit_heads * HD
    factor = math.log2(math.e) / math.sqrt(HD)

    z = lax.axis_index("span")
    me = lax.axis_index("head")
    chip, core = me // CORES, me % CORES
    sibling = chip * CORES + (1 - core)

    barrier = pltpu.get_barrier_semaphore()
    for step in range(1, peers):
        pl.semaphore_signal(
            barrier, inc=1, device_id={"head": (me + step) % peers}, device_id_type=MESH
        )

    @pl.when(z > 0)
    def _():
        for other in (me, sibling):
            pl.semaphore_signal(
                barrier, inc=1, device_id={"span": z - 1, "head": other}, device_id_type=MESH
            )

    def lanes_of(owner, unit, width):
        start = (owner * units + unit) * width
        return pl.ds(pl.multiple_of(start, width), width)

    def piece(kv, owner, unit):
        return (k_hbm, v_hbm)[kv].at[:, lanes_of(owner, unit, unit_width)]

    def place(level, unit, slot, kv):
        return kv_buf.at[level, unit, slot, kv, core]

    def half(ref, owner):
        return ref.at[:, pl.ds(pl.multiple_of(owner * heads * HD, heads * HD), heads * HD)]

    loads = [
        pltpu.make_async_copy(source, target, load_sem.at[n])
        for n, (source, target) in enumerate(
            (
                (frames_hbm, frames_ref),
                (noise_hbm, noise_ref),
                (mask_hbm, mask_ref),
                (gate_hbm, gate_ref),
                (half(q_hbm, core), q_ref.at[core]),
            )
        )
    ]
    for load in loads:
        load.start()
    own = [
        pltpu.make_async_copy(piece(kv, core, u), place(z, u, chip, kv), own_sem.at[u, kv])
        for u in range(units)
        for kv in range(2)
    ]
    for load in own:
        load.start()

    pl.semaphore_wait(barrier, peers - 1 + jnp.where(z < levels - 1, CORES, 0))

    def send(source, target, send_sem, arrive_sem, device):
        return pltpu.make_async_remote_copy(
            src_ref=source,
            dst_ref=target,
            send_sem=send_sem,
            recv_sem=arrive_sem,
            device_id=device,
            device_id_type=MESH,
        )

    def first(unit, kv, turn, hop):
        owner = core if turn == 0 else 1 - core
        target = place(z, unit, chip, kv)
        if hop == "up":
            device = {"span": z + 1, "head": chip * CORES + owner}
            index = 0
        else:
            device = {"head": ((chip + hop) % chips) * CORES + owner}
            index = 1 + hop
        return send(
            piece(kv, owner, unit), target, first_sem.at[unit, kv, turn, index],
            recv_sem.at[z, unit, chip], device,
        )

    def first_copies(unit, turn):
        hops = list(range(1, chips)) + ([0] if turn else [])
        return [first(unit, kv, turn, hop) for hop in hops for kv in range(2)]

    def first_up(unit, turn):
        return [first(unit, kv, turn, "up") for kv in range(2)]

    def up(level, unit):
        slot = kv_buf.at[level, unit, chip]
        return send(
            slot, slot, up_sem.at[level, unit], recv_sem.at[level, unit, chip], {"span": z + 1}
        )

    def across(level, unit, step):
        slot = kv_buf.at[level, unit, chip]
        return send(
            slot, slot, across_sem.at[level, unit, step - 1], recv_sem.at[level, unit, chip],
            {"head": ((chip + step) % chips) * CORES + core},
        )

    def wait_slot(level, unit, slot):
        whole = kv_buf.at[level, unit, slot]
        send(
            whole, whole, up_sem.at[level, unit], recv_sem.at[level, unit, slot],
            {"head": sibling},
        ).wait_recv()

    def wait_sibling(unit):
        rest = kv_buf.at[z, unit, chip, :, 1 - core]
        send(
            rest, rest, up_sem.at[z, unit], recv_sem.at[z, unit, chip], {"head": sibling}
        ).wait_recv()

    def issue(level, unit):
        @pl.when(z < levels - 1)
        def _():
            up(level, unit).start()

        for step in range(1, chips):
            across(level, unit, step).start()

    swap = send(
        half(q_hbm, 1 - core), q_ref.at[core], q_send.at[0], q_recv.at[0], {"head": sibling}
    )

    def gate_copy(step):
        target = (me + step) % peers
        return send(
            gate_out.at[(target * rows) // CT], gate_in.at[me],
            gate_send.at[step], gate_recv.at[me], {"head": target},
        )

    for u in range(units):
        for turn in range(2):
            @pl.when(z < levels - 1)
            def _():
                for one in first_up(u, turn):
                    one.start()

            for one in first_copies(u, turn):
                one.start()
        if u == 0:
            swap.start()

    acc[...] = jnp.zeros_like(acc)
    top[...] = jnp.full_like(top, LOW)
    for load in loads:
        load.wait()
    for i in range(level_spans):
        level_index = noise_ref[z * level_spans + i]
        pick = lax.broadcasted_iota(jnp.int32, (8, gate_ref.shape[0]), 1) == level_index
        picked = jnp.dot(
            pick.astype(jnp.bfloat16), gate_ref[...], preferred_element_type=jnp.float32
        )
        for n in range(heads_dev):
            gate_out[i, n : n + 1, :] = picked[0:1, n * HD : (n + 1) * HD]
    for step in range(1, peers):
        gate_copy(step).start()

    token = chip * chip_rows
    span = z * level_spans + token // CT
    gate_in[me] = gate_out[token // CT]
    for load in own:
        load.wait()
    send(
        q_ref.at[1 - core], q_ref.at[1 - core], q_send.at[0], q_recv.at[0], {"head": sibling}
    ).wait_recv()
    for step in range(1, peers):
        source = (me + step) % peers
        send(
            gate_out.at[0], gate_in.at[source], gate_send.at[step], gate_recv.at[source],
            {"head": source},
        ).wait_recv()

    def fold(level, unit):
        column = lax.broadcasted_iota(jnp.int32, (1, level_rows), 1)
        usable = column < 0
        for i in range(level_spans):
            key_span = level * level_spans + i
            limit = jnp.where(mask_ref[span, key_span] > 0, frames_ref[key_span] * FRAME_TOK, 0)
            usable = usable | ((column >= i * CT) & (column < i * CT + limit))
        bias = jnp.where(usable, jnp.float32(0.0), jnp.float32(LOW))
        ones = jnp.ones((level_rows, HD), jnp.bfloat16)

        for n in range(unit_heads):
            j = unit * unit_heads + n
            lanes = slice(n * HD, (n + 1) * HD)
            queries = jnp.concatenate(
                [
                    q_ref[:, :, (j * group + g) * HD : (j * group + g + 1) * HD].reshape(
                        chip_rows, HD
                    )
                    for g in range(group)
                ],
                axis=0,
            )
            keys = kv_buf[level, unit, :, 0, :, :, lanes].reshape(level_rows, HD)
            values = kv_buf[level, unit, :, 1, :, :, lanes].reshape(level_rows, HD)
            scores = lax.dot_general(
                queries, keys, (((1,), (1,)), ((), ())), preferred_element_type=jnp.float32
            )
            scores = scores + bias
            old = top[j]
            new = jnp.maximum(old, jnp.max(scores, axis=1, keepdims=True))
            top[j] = new
            weights = jnp.exp2((scores - new[:, :1]) * factor).astype(jnp.bfloat16)
            update = jnp.dot(
                weights,
                jnp.concatenate([values, ones], axis=1),
                preferred_element_type=jnp.float32,
            )
            shrink = jnp.exp2((old - new) * factor)
            acc[j] = acc[j] * jnp.concatenate([shrink, shrink], axis=1) + update

    position = token % CT + lax.broadcasted_iota(jnp.int32, (chip_rows, HD), 0)
    live = position < frames_ref[span] * FRAME_TOK
    out_width = unit_width * group

    def out_lanes(owner, unit):
        return out_hbm.at[:, lanes_of(owner, unit, out_width)]

    def out_own(unit):
        return pltpu.make_async_copy(
            stage.at[unit, core], out_lanes(core, unit), out_sem.at[unit]
        )

    def out_swap(unit):
        return send(
            stage.at[unit, 1 - core], out_lanes(core, unit),
            out_send.at[unit], out_recv.at[unit], {"head": sibling},
        )

    def finish(unit):
        for n in range(unit_heads):
            j = unit * unit_heads + n
            for g in range(group):
                head = j * group + g
                part = slice(g * chip_rows, (g + 1) * chip_rows)
                row = head % heads_dev
                gate = gate_in[core * (peers // CORES) + head // heads_dev, row : row + 1, :]
                ratio = acc[j, part, :HD] / acc[j, part, HD:]
                done = jnp.where(live, ratio * gate, jnp.float32(0.0)).astype(stage.dtype)
                at = slice((n * group + g) * HD, (n * group + g + 1) * HD)
                stage[unit, :, :, at] = done.reshape(CORES, rows, HD)
        out_swap(unit).start()
        out_own(unit).start()

    def one_level(s, carry):
        level = z - s
        for u in range(units):
            ahead, ahead_unit = (u + 1) // units, (u + 1) % units

            @pl.when((s >= 1) if ahead == 0 else (s + ahead <= z))
            def _():
                wait_slot(level - ahead, ahead_unit, chip)
                issue(level - ahead, ahead_unit)

            @pl.when(s == 0)
            def _():
                wait_sibling(u)

            for step in range(1, chips):
                wait_slot(level, u, (chip + step) % chips)
            fold(level, u)

            @pl.when(s == z)
            def _():
                finish(u)
        return carry

    lax.fori_loop(0, z + 1, one_level, 0)

    for u in range(units):
        for turn in range(2):
            @pl.when(z < levels - 1)
            def _():
                for one in first_up(u, turn):
                    one.wait_send()

            for one in first_copies(u, turn):
                one.wait_send()

    def drain(s, carry):
        level = z - s
        for u in range(units):
            @pl.when(z < levels - 1)
            def _():
                up(level, u).wait_send()

            for step in range(1, chips):
                across(level, u, step).wait_send()
        return carry

    lax.fori_loop(1, z + 1, drain, 0)
    swap.wait_send()
    for step in range(1, peers):
        gate_copy(step).wait_send()
    for u in range(units):
        out_own(u).wait()
        out_swap(u).wait_send()
        send(
            stage.at[u, 1 - core], out_lanes(1 - core, u),
            out_send.at[u], out_recv.at[u], {"head": sibling},
        ).wait_recv()


def body(levels, peers, q, k, v, frames, noise, mask, gate):
    rows, kv_width = k.shape
    kv_heads = kv_width // HD // CORES
    group_rows = q.shape[1] // kv_width * rows * CORES
    chips = peers // CORES
    units = kv_heads // 2
    level_spans = peers * rows // CT
    gate_rows = -(-(gate.shape[1] // HD) // 8) * 8
    hbm = pl.BlockSpec(memory_space=pltpu.HBM)
    pairs = q.shape[0] * q.shape[1] // HD * levels * peers * rows
    unit_width = kv_width // CORES // units
    out_width = q.shape[1] // CORES // units
    return pl.pallas_call(
        functools.partial(kernel, levels, peers, units),
        out_shape=jax.ShapeDtypeStruct(q.shape, q.dtype),
        in_specs=[hbm] * 7,
        out_specs=hbm,
        scratch_shapes=[
            pltpu.VMEM((levels, units, chips, 2, CORES, rows, unit_width), k.dtype),
            pltpu.VMEM((CORES, rows, q.shape[1] // CORES), q.dtype),
            pltpu.VMEM((units, CORES, rows, out_width), q.dtype),
            pltpu.VMEM(gate.shape, gate.dtype),
            pltpu.SMEM(frames.shape, frames.dtype),
            pltpu.SMEM(noise.shape, noise.dtype),
            pltpu.SMEM(mask.shape, mask.dtype),
            pltpu.VMEM((kv_heads, group_rows, 2 * HD), jnp.float32),
            pltpu.VMEM((kv_heads, group_rows, HD), jnp.float32),
            pltpu.VMEM((level_spans, gate_rows, HD), jnp.float32),
            pltpu.VMEM((peers, gate_rows, HD), jnp.float32),
            pltpu.SemaphoreType.DMA((levels, units, chips)),
            pltpu.SemaphoreType.DMA((units, 2, 2, chips + 1)),
            pltpu.SemaphoreType.DMA((levels, units)),
            pltpu.SemaphoreType.DMA((levels, units, max(chips - 1, 1))),
            pltpu.SemaphoreType.DMA((peers,)),
            pltpu.SemaphoreType.DMA((peers,)),
            pltpu.SemaphoreType.DMA((units, 2)),
            pltpu.SemaphoreType.DMA((5,)),
            pltpu.SemaphoreType.DMA((1,)),
            pltpu.SemaphoreType.DMA((1,)),
            pltpu.SemaphoreType.DMA((units,)),
            pltpu.SemaphoreType.DMA((units,)),
            pltpu.SemaphoreType.DMA((units,)),
        ],
        compiler_params=pltpu.CompilerParams(
            collective_id=0, has_side_effects=True, vmem_limit_bytes=64 << 20
        ),
        cost_estimate=pl.CostEstimate(
            flops=pairs * HD * 4, bytes_accessed=4 * q.size, transcendentals=pairs
        ),
    )(q, k, v, frames, noise, mask, gate)


def solution(mesh):
    placed = (
        P(("groups", "span", "head"), None),
        P(("groups", "span", "head"), None),
        P(("groups", "span", "head"), None),
        P("groups"),
        P("groups"),
        P("groups", None),
        P(None, "head"),
    )
    return jax.shard_map(
        functools.partial(body, mesh.shape["span"], mesh.shape["head"]),
        mesh=mesh,
        in_specs=placed,
        out_specs=P(("groups", "span", "head"), None),
        check_vma=False,
    )
```

```python
import functools
import math

import jax
import jax.numpy as jnp
from jax import lax
from jax.experimental import pallas as pl
from jax.experimental.pallas import tpu as pltpu
from jax.sharding import PartitionSpec as P

HD = 128
FRAME_TOK = 32
CT = 128
CORES = 2
PAIR = 2
MESH = pl.DeviceIdType.MESH
LOW = -1e30


def kernel(
    levels, peers, units,
    q_hbm, k_hbm, v_hbm, frames_hbm, noise_hbm, mask_hbm, gate_hbm,
    out_hbm,
    kv_buf, q_ref, stage, gate_ref, frames_ref, noise_ref, mask_ref, acc, top, gate_out, gate_in,
    recv_sem, first_sem, up_sem, across_sem, gate_send, gate_recv, own_sem, load_sem,
    q_send, q_recv, out_send, out_recv, out_sem,
):
    rows, kv_width = k_hbm.shape
    kv_heads = kv_width // HD // CORES
    heads = q_hbm.shape[1] // HD // CORES
    group = heads // kv_heads
    heads_dev = gate_hbm.shape[1] // HD
    chips = peers // CORES
    chip_rows = CORES * rows
    level_rows = peers * rows
    level_spans = level_rows // CT
    unit_heads = kv_heads // units
    unit_width = unit_heads * HD
    tile = PAIR * chip_rows
    factor = math.log2(math.e) / math.sqrt(HD)

    z = lax.axis_index("span")
    me = lax.axis_index("head")
    chip, core = me // CORES, me % CORES
    sibling = chip * CORES + (1 - core)

    barrier = pltpu.get_barrier_semaphore()
    for step in range(1, peers):
        pl.semaphore_signal(
            barrier, inc=1, device_id={"head": (me + step) % peers}, device_id_type=MESH
        )

    @pl.when(z > 0)
    def _():
        for other in (me, sibling):
            pl.semaphore_signal(
                barrier, inc=1, device_id={"span": z - 1, "head": other}, device_id_type=MESH
            )

    def lanes_of(owner, unit, width):
        start = (owner * units + unit) * width
        return pl.ds(pl.multiple_of(start, width), width)

    def piece(kv, owner, unit):
        return (k_hbm, v_hbm)[kv].at[:, lanes_of(owner, unit, unit_width)]

    def place(level, unit, slot, kv):
        return kv_buf.at[level, unit, slot, kv, core]

    def half(ref, owner):
        return ref.at[:, pl.ds(pl.multiple_of(owner * heads * HD, heads * HD), heads * HD)]

    loads = [
        pltpu.make_async_copy(source, target, load_sem.at[n])
        for n, (source, target) in enumerate(
            (
                (frames_hbm, frames_ref),
                (noise_hbm, noise_ref),
                (mask_hbm, mask_ref),
                (gate_hbm, gate_ref),
                (half(q_hbm, core), q_ref.at[core]),
            )
        )
    ]
    for load in loads:
        load.start()
    own = [
        pltpu.make_async_copy(piece(kv, core, u), place(z, u, chip, kv), own_sem.at[u, kv])
        for u in range(units)
        for kv in range(2)
    ]
    for load in own:
        load.start()

    pl.semaphore_wait(barrier, peers - 1 + jnp.where(z < levels - 1, CORES, 0))

    def send(source, target, send_sem, arrive_sem, device):
        return pltpu.make_async_remote_copy(
            src_ref=source,
            dst_ref=target,
            send_sem=send_sem,
            recv_sem=arrive_sem,
            device_id=device,
            device_id_type=MESH,
        )

    def first(unit, kv, turn, hop):
        owner = core if turn == 0 else 1 - core
        target = place(z, unit, chip, kv)
        if hop == "up":
            device = {"span": z + 1, "head": chip * CORES + owner}
            index = 0
        else:
            device = {"head": ((chip + hop) % chips) * CORES + owner}
            index = 1 + hop
        return send(
            piece(kv, owner, unit), target, first_sem.at[unit, kv, turn, index],
            recv_sem.at[z, unit, chip], device,
        )

    def first_copies(unit, turn):
        hops = list(range(1, chips)) + ([0] if turn else [])
        return [first(unit, kv, turn, hop) for hop in hops for kv in range(2)]

    def first_up(unit, turn):
        return [first(unit, kv, turn, "up") for kv in range(2)]

    def up(level, unit):
        slot = kv_buf.at[level, unit, chip]
        return send(
            slot, slot, up_sem.at[level, unit], recv_sem.at[level, unit, chip], {"span": z + 1}
        )

    def across(level, unit, step):
        slot = kv_buf.at[level, unit, chip]
        return send(
            slot, slot, across_sem.at[level, unit, step - 1], recv_sem.at[level, unit, chip],
            {"head": ((chip + step) % chips) * CORES + core},
        )

    def wait_slot(level, unit, slot):
        whole = kv_buf.at[level, unit, slot]
        send(
            whole, whole, up_sem.at[level, unit], recv_sem.at[level, unit, slot],
            {"head": sibling},
        ).wait_recv()

    def wait_sibling(unit):
        rest = kv_buf.at[z, unit, chip, :, 1 - core]
        send(
            rest, rest, up_sem.at[z, unit], recv_sem.at[z, unit, chip], {"head": sibling}
        ).wait_recv()

    def issue(level, unit):
        @pl.when(z < levels - 1)
        def _():
            up(level, unit).start()

        for step in range(1, chips):
            across(level, unit, step).start()

    swap = send(
        half(q_hbm, 1 - core), q_ref.at[core], q_send.at[0], q_recv.at[0], {"head": sibling}
    )

    def gate_copy(step):
        target = (me + step) % peers
        return send(
            gate_out.at[(target * rows) // CT], gate_in.at[me],
            gate_send.at[step], gate_recv.at[me], {"head": target},
        )

    for u in range(units):
        for turn in range(2):
            @pl.when(z < levels - 1)
            def _():
                for one in first_up(u, turn):
                    one.start()

            for one in first_copies(u, turn):
                one.start()
        if u == 0:
            swap.start()

    acc[...] = jnp.zeros_like(acc)
    top[:, 0:1, :] = jnp.full((kv_heads, 1, top.shape[2]), LOW, jnp.float32)
    top[:, 1:2, :] = jnp.zeros((kv_heads, 1, top.shape[2]), jnp.float32)
    for load in loads:
        load.wait()
    for i in range(level_spans):
        level_index = noise_ref[z * level_spans + i]
        pick = lax.broadcasted_iota(jnp.int32, (8, gate_ref.shape[0]), 1) == level_index
        picked = jnp.dot(
            pick.astype(jnp.bfloat16), gate_ref[...], preferred_element_type=jnp.float32
        )
        for n in range(heads_dev):
            gate_out[i, n : n + 1, :] = picked[0:1, n * HD : (n + 1) * HD]
    for step in range(1, peers):
        gate_copy(step).start()

    token = chip * chip_rows
    span = z * level_spans + token // CT
    gate_in[me] = gate_out[token // CT]
    for load in own:
        load.wait()
    send(
        q_ref.at[1 - core], q_ref.at[1 - core], q_send.at[0], q_recv.at[0], {"head": sibling}
    ).wait_recv()
    for step in range(1, peers):
        source = (me + step) % peers
        send(
            gate_out.at[0], gate_in.at[source], gate_send.at[step], gate_recv.at[source],
            {"head": source},
        ).wait_recv()

    def fold(level, unit):
        row = lax.broadcasted_iota(jnp.int32, (level_rows, tile), 0)
        usable = row < 0
        for i in range(level_spans):
            key_span = level * level_spans + i
            limit = jnp.where(mask_ref[span, key_span] > 0, frames_ref[key_span] * FRAME_TOK, 0)
            usable = usable | ((row >= i * CT) & (row < i * CT + limit))
        bias = jnp.where(usable, jnp.float32(0.0), jnp.float32(LOW))

        def score(n, t):
            j = unit * unit_heads + n
            queries = jnp.concatenate(
                [
                    q_ref[:, :, (j * group + g) * HD : (j * group + g + 1) * HD].reshape(
                        chip_rows, HD
                    )
                    for g in range(t * PAIR, (t + 1) * PAIR)
                ],
                axis=0,
            )
            keys = kv_buf[level, unit, :, 0, :, :, n * HD : (n + 1) * HD].reshape(level_rows, HD)
            return lax.dot_general(
                keys, queries, (((1,), (1,)), ((), ())), preferred_element_type=jnp.float32
            )

        steps = [(n, t) for n in range(unit_heads) for t in range(group // PAIR)]
        ready = score(*steps[0])
        for at, (n, t) in enumerate(steps):
            scores = ready + bias
            if at + 1 < len(steps):
                ready = score(*steps[at + 1])
            j = unit * unit_heads + n
            lanes = slice(t * tile, (t + 1) * tile)
            if t == 0:
                values = kv_buf[level, unit, :, 1, :, :, n * HD : (n + 1) * HD]
                values = values.reshape(level_rows, HD).T
            old = top[j, 0:1, lanes]
            new = jnp.maximum(old, jnp.max(scores, axis=0, keepdims=True))
            top[j, 0:1, lanes] = new
            weights = jnp.exp2((scores - new) * factor)
            shrink = jnp.exp2((old - new) * factor)
            top[j, 1:2, lanes] = top[j, 1:2, lanes] * shrink + jnp.sum(
                weights, axis=0, keepdims=True
            )
            update = jnp.dot(
                values, weights.astype(jnp.bfloat16), preferred_element_type=jnp.float32
            )
            acc[j, :, lanes] = acc[j, :, lanes] * shrink + update

    position = token % CT + lax.broadcasted_iota(jnp.int32, (chip_rows, HD), 0)
    live = position < frames_ref[span] * FRAME_TOK
    out_width = unit_width * group

    def out_lanes(owner, unit):
        return out_hbm.at[:, lanes_of(owner, unit, out_width)]

    def out_own(unit):
        return pltpu.make_async_copy(
            stage.at[unit, core], out_lanes(core, unit), out_sem.at[unit]
        )

    def out_swap(unit):
        return send(
            stage.at[unit, 1 - core], out_lanes(core, unit),
            out_send.at[unit], out_recv.at[unit], {"head": sibling},
        )

    def finish(unit):
        for n in range(unit_heads):
            j = unit * unit_heads + n
            for t in range(group // PAIR):
                lanes = slice(t * tile, (t + 1) * tile)
                ratio = (acc[j, :, lanes] / top[j, 1:2, lanes]).T
                for g in range(t * PAIR, (t + 1) * PAIR):
                    head = j * group + g
                    row = head % heads_dev
                    gate = gate_in[core * (peers // CORES) + head // heads_dev, row : row + 1, :]
                    part = ratio[(g - t * PAIR) * chip_rows : (g - t * PAIR + 1) * chip_rows]
                    done = jnp.where(live, part * gate, jnp.float32(0.0)).astype(stage.dtype)
                    at = slice((n * group + g) * HD, (n * group + g + 1) * HD)
                    stage[unit, :, :, at] = done.reshape(CORES, rows, HD)
        out_swap(unit).start()
        out_own(unit).start()

    def one_level(s, carry):
        level = z - s
        for u in range(units):
            ahead, ahead_unit = (u + 1) // units, (u + 1) % units

            @pl.when((s >= 1) if ahead == 0 else (s + ahead <= z))
            def _():
                wait_slot(level - ahead, ahead_unit, chip)
                issue(level - ahead, ahead_unit)

            @pl.when(s == 0)
            def _():
                wait_sibling(u)

            for step in range(1, chips):
                wait_slot(level, u, (chip + step) % chips)
            fold(level, u)

            @pl.when(s == z)
            def _():
                finish(u)
        return carry

    lax.fori_loop(0, z + 1, one_level, 0)

    for u in range(units):
        for turn in range(2):
            @pl.when(z < levels - 1)
            def _():
                for one in first_up(u, turn):
                    one.wait_send()

            for one in first_copies(u, turn):
                one.wait_send()

    def drain(s, carry):
        level = z - s
        for u in range(units):
            @pl.when(z < levels - 1)
            def _():
                up(level, u).wait_send()

            for step in range(1, chips):
                across(level, u, step).wait_send()
        return carry

    lax.fori_loop(1, z + 1, drain, 0)
    swap.wait_send()
    for step in range(1, peers):
        gate_copy(step).wait_send()
    for u in range(units):
        out_own(u).wait()
        out_swap(u).wait_send()
        send(
            stage.at[u, 1 - core], out_lanes(1 - core, u),
            out_send.at[u], out_recv.at[u], {"head": sibling},
        ).wait_recv()


def body(levels, peers, q, k, v, frames, noise, mask, gate):
    rows, kv_width = k.shape
    kv_heads = kv_width // HD // CORES
    group_rows = q.shape[1] // kv_width * rows * CORES
    chips = peers // CORES
    units = kv_heads // 2
    level_spans = peers * rows // CT
    gate_rows = -(-(gate.shape[1] // HD) // 8) * 8
    hbm = pl.BlockSpec(memory_space=pltpu.HBM)
    pairs = q.shape[0] * q.shape[1] // HD * levels * peers * rows
    unit_width = kv_width // CORES // units
    out_width = q.shape[1] // CORES // units
    return pl.pallas_call(
        functools.partial(kernel, levels, peers, units),
        out_shape=jax.ShapeDtypeStruct(q.shape, q.dtype),
        in_specs=[hbm] * 7,
        out_specs=hbm,
        scratch_shapes=[
            pltpu.VMEM((levels, units, chips, 2, CORES, rows, unit_width), k.dtype),
            pltpu.VMEM((CORES, rows, q.shape[1] // CORES), q.dtype),
            pltpu.VMEM((units, CORES, rows, out_width), q.dtype),
            pltpu.VMEM(gate.shape, gate.dtype),
            pltpu.SMEM(frames.shape, frames.dtype),
            pltpu.SMEM(noise.shape, noise.dtype),
            pltpu.SMEM(mask.shape, mask.dtype),
            pltpu.VMEM((kv_heads, HD, group_rows), jnp.float32),
            pltpu.VMEM((kv_heads, 2, group_rows), jnp.float32),
            pltpu.VMEM((level_spans, gate_rows, HD), jnp.float32),
            pltpu.VMEM((peers, gate_rows, HD), jnp.float32),
            pltpu.SemaphoreType.DMA((levels, units, chips)),
            pltpu.SemaphoreType.DMA((units, 2, 2, chips + 1)),
            pltpu.SemaphoreType.DMA((levels, units)),
            pltpu.SemaphoreType.DMA((levels, units, max(chips - 1, 1))),
            pltpu.SemaphoreType.DMA((peers,)),
            pltpu.SemaphoreType.DMA((peers,)),
            pltpu.SemaphoreType.DMA((units, 2)),
            pltpu.SemaphoreType.DMA((5,)),
            pltpu.SemaphoreType.DMA((1,)),
            pltpu.SemaphoreType.DMA((1,)),
            pltpu.SemaphoreType.DMA((units,)),
            pltpu.SemaphoreType.DMA((units,)),
            pltpu.SemaphoreType.DMA((units,)),
        ],
        compiler_params=pltpu.CompilerParams(
            collective_id=0, has_side_effects=True, vmem_limit_bytes=64 << 20
        ),
        cost_estimate=pl.CostEstimate(
            flops=pairs * HD * 4, bytes_accessed=4 * q.size, transcendentals=pairs
        ),
    )(q, k, v, frames, noise, mask, gate)


def solution(mesh):
    placed = (
        P(("groups", "span", "head"), None),
        P(("groups", "span", "head"), None),
        P(("groups", "span", "head"), None),
        P("groups"),
        P("groups"),
        P("groups", None),
        P(None, "head"),
    )
    return jax.shard_map(
        functools.partial(body, mesh.shape["span"], mesh.shape["head"]),
        mesh=mesh,
        in_specs=placed,
        out_specs=P(("groups", "span", "head"), None),
        check_vma=False,
    )
```

```python
import functools
import math

import jax
import jax.numpy as jnp
from jax import lax
from jax.experimental import pallas as pl
from jax.experimental.pallas import tpu as pltpu
from jax.sharding import PartitionSpec as P

HD = 128
FRAME_TOK = 32
CT = 128
CORES = 2
MESH = pl.DeviceIdType.MESH
LOW = -1e30


def kernel(
    levels, peers, units,
    q_hbm, k_hbm, v_hbm, frames_hbm, noise_hbm, mask_hbm, gate_hbm,
    out_hbm,
    kv_buf, q_ref, stage, gate_ref, frames_ref, noise_ref, mask_ref, acc, top, gate_out, gate_in,
    recv_sem, first_sem, up_sem, across_sem, gate_send, gate_recv, own_sem, load_sem,
    q_send, q_recv, out_send, out_recv, out_sem,
):
    rows, kv_width = k_hbm.shape
    kv_heads = kv_width // HD // CORES
    heads = q_hbm.shape[1] // HD // CORES
    group = heads // kv_heads
    heads_dev = gate_hbm.shape[1] // HD
    chips = peers // CORES
    chip_rows = CORES * rows
    level_rows = peers * rows
    level_spans = level_rows // CT
    unit_heads = kv_heads // units
    unit_width = unit_heads * HD
    factor = math.log2(math.e) / math.sqrt(HD)

    z = lax.axis_index("span")
    me = lax.axis_index("head")
    chip, core = me // CORES, me % CORES
    sibling = chip * CORES + (1 - core)

    barrier = pltpu.get_barrier_semaphore()
    for step in range(1, peers):
        pl.semaphore_signal(
            barrier, inc=1, device_id={"head": (me + step) % peers}, device_id_type=MESH
        )

    @pl.when(z > 0)
    def _():
        for other in (me, sibling):
            pl.semaphore_signal(
                barrier, inc=1, device_id={"span": z - 1, "head": other}, device_id_type=MESH
            )

    def lanes_of(owner, unit, width):
        start = (owner * units + unit) * width
        return pl.ds(pl.multiple_of(start, width), width)

    def piece(kv, owner, unit):
        return (k_hbm, v_hbm)[kv].at[:, lanes_of(owner, unit, unit_width)]

    def place(level, unit, slot, kv):
        return kv_buf.at[level, unit, slot, kv, core]

    def half(ref, owner):
        return ref.at[:, pl.ds(pl.multiple_of(owner * heads * HD, heads * HD), heads * HD)]

    loads = [
        pltpu.make_async_copy(source, target, load_sem.at[n])
        for n, (source, target) in enumerate(
            (
                (frames_hbm, frames_ref),
                (noise_hbm, noise_ref),
                (mask_hbm, mask_ref),
                (gate_hbm, gate_ref),
                (half(q_hbm, core), q_ref.at[core]),
            )
        )
    ]
    for load in loads:
        load.start()
    own = [
        pltpu.make_async_copy(piece(kv, core, u), place(z, u, chip, kv), own_sem.at[u, kv])
        for u in range(units)
        for kv in range(2)
    ]
    for load in own:
        load.start()

    pl.semaphore_wait(barrier, peers - 1 + jnp.where(z < levels - 1, CORES, 0))

    def send(source, target, send_sem, arrive_sem, device):
        return pltpu.make_async_remote_copy(
            src_ref=source,
            dst_ref=target,
            send_sem=send_sem,
            recv_sem=arrive_sem,
            device_id=device,
            device_id_type=MESH,
        )

    def first(unit, kv, turn, hop):
        owner = core if turn == 0 else 1 - core
        target = place(z, unit, chip, kv)
        if hop == "up":
            device = {"span": z + 1, "head": chip * CORES + owner}
            index = 0
        else:
            device = {"head": ((chip + hop) % chips) * CORES + owner}
            index = 1 + hop
        return send(
            piece(kv, owner, unit), target, first_sem.at[unit, kv, turn, index],
            recv_sem.at[z, unit, chip], device,
        )

    def first_copies(unit, turn):
        hops = list(range(1, chips)) + ([0] if turn else [])
        return [first(unit, kv, turn, hop) for hop in hops for kv in range(2)]

    def first_up(unit, turn):
        return [first(unit, kv, turn, "up") for kv in range(2)]

    def up(level, unit):
        slot = kv_buf.at[level, unit, chip]
        return send(
            slot, slot, up_sem.at[level, unit], recv_sem.at[level, unit, chip], {"span": z + 1}
        )

    def across(level, unit, step):
        slot = kv_buf.at[level, unit, chip]
        return send(
            slot, slot, across_sem.at[level, unit, step - 1], recv_sem.at[level, unit, chip],
            {"head": ((chip + step) % chips) * CORES + core},
        )

    def wait_slot(level, unit, slot):
        whole = kv_buf.at[level, unit, slot]
        send(
            whole, whole, up_sem.at[level, unit], recv_sem.at[level, unit, slot],
            {"head": sibling},
        ).wait_recv()

    def wait_sibling(unit):
        rest = kv_buf.at[z, unit, chip, :, 1 - core]
        send(
            rest, rest, up_sem.at[z, unit], recv_sem.at[z, unit, chip], {"head": sibling}
        ).wait_recv()

    def issue(level, unit):
        @pl.when(z < levels - 1)
        def _():
            up(level, unit).start()

        for step in range(1, chips):
            across(level, unit, step).start()

    swap = send(
        half(q_hbm, 1 - core), q_ref.at[core], q_send.at[0], q_recv.at[0], {"head": sibling}
    )

    def gate_copy(step):
        target = (me + step) % peers
        return send(
            gate_out.at[(target * rows) // CT], gate_in.at[me],
            gate_send.at[step], gate_recv.at[me], {"head": target},
        )

    for u in range(units):
        for turn in range(2):
            @pl.when(z < levels - 1)
            def _():
                for one in first_up(u, turn):
                    one.start()

            for one in first_copies(u, turn):
                one.start()
        if u == 0:
            swap.start()

    acc[...] = jnp.zeros_like(acc)
    top[...] = jnp.full_like(top, LOW)
    for load in loads:
        load.wait()
    for i in range(level_spans):
        level_index = noise_ref[z * level_spans + i]
        pick = lax.broadcasted_iota(jnp.int32, (8, gate_ref.shape[0]), 1) == level_index
        picked = jnp.dot(
            pick.astype(jnp.bfloat16), gate_ref[...], preferred_element_type=jnp.float32
        )
        for n in range(heads_dev):
            gate_out[i, n : n + 1, :] = picked[0:1, n * HD : (n + 1) * HD]
    for step in range(1, peers):
        gate_copy(step).start()

    token = chip * chip_rows
    span = z * level_spans + token // CT
    gate_in[me] = gate_out[token // CT]
    for load in own:
        load.wait()
    send(
        q_ref.at[1 - core], q_ref.at[1 - core], q_send.at[0], q_recv.at[0], {"head": sibling}
    ).wait_recv()
    for step in range(1, peers):
        source = (me + step) % peers
        send(
            gate_out.at[0], gate_in.at[source], gate_send.at[step], gate_recv.at[source],
            {"head": source},
        ).wait_recv()

    def fold(level, unit):
        column = lax.broadcasted_iota(jnp.int32, (1, level_rows), 1)
        usable = column < 0
        for i in range(level_spans):
            key_span = level * level_spans + i
            limit = jnp.where(mask_ref[span, key_span] > 0, frames_ref[key_span] * FRAME_TOK, 0)
            usable = usable | ((column >= i * CT) & (column < i * CT + limit))
        bias = jnp.where(usable, jnp.float32(0.0), jnp.float32(LOW))
        ones = jnp.ones((level_rows, HD), jnp.bfloat16)

        for n in range(unit_heads):
            j = unit * unit_heads + n
            lanes = slice(n * HD, (n + 1) * HD)
            queries = jnp.concatenate(
                [
                    q_ref[:, :, (j * group + g) * HD : (j * group + g + 1) * HD].reshape(
                        chip_rows, HD
                    )
                    for g in range(group)
                ],
                axis=0,
            )
            keys = kv_buf[level, unit, :, 0, :, :, lanes].reshape(level_rows, HD)
            values = kv_buf[level, unit, :, 1, :, :, lanes].reshape(level_rows, HD)
            scores = lax.dot_general(
                queries, keys, (((1,), (1,)), ((), ())), preferred_element_type=jnp.float32
            )
            scores = scores + bias
            old = top[j]
            new = jnp.maximum(old, jnp.max(scores, axis=1, keepdims=True))
            top[j] = new
            wide = jnp.concatenate([new] * (level_rows // HD), axis=1)
            weights = jnp.exp2((scores - wide) * factor).astype(jnp.bfloat16)
            update = jnp.dot(
                weights,
                jnp.concatenate([values, ones], axis=1),
                preferred_element_type=jnp.float32,
            )
            shrink = jnp.exp2((old - new) * factor)
            acc[j] = acc[j] * jnp.concatenate([shrink, shrink], axis=1) + update

    position = token % CT + lax.broadcasted_iota(jnp.int32, (chip_rows, HD), 0)
    live = position < frames_ref[span] * FRAME_TOK
    out_width = unit_width * group

    def out_lanes(owner, unit):
        return out_hbm.at[:, lanes_of(owner, unit, out_width)]

    def out_own(unit):
        return pltpu.make_async_copy(
            stage.at[unit, core], out_lanes(core, unit), out_sem.at[unit]
        )

    def out_swap(unit):
        return send(
            stage.at[unit, 1 - core], out_lanes(core, unit),
            out_send.at[unit], out_recv.at[unit], {"head": sibling},
        )

    def finish(unit):
        for n in range(unit_heads):
            j = unit * unit_heads + n
            for g in range(group):
                head = j * group + g
                part = slice(g * chip_rows, (g + 1) * chip_rows)
                row = head % heads_dev
                gate = gate_in[core * (peers // CORES) + head // heads_dev, row : row + 1, :]
                ratio = acc[j, part, :HD] / acc[j, part, HD:]
                done = jnp.where(live, ratio * gate, jnp.float32(0.0)).astype(stage.dtype)
                at = slice((n * group + g) * HD, (n * group + g + 1) * HD)
                stage[unit, :, :, at] = done.reshape(CORES, rows, HD)
        out_swap(unit).start()
        out_own(unit).start()

    def one_level(s, carry):
        level = z - s
        for u in range(units):
            @pl.when(s < z)
            def _():
                wait_slot(level - 1, u, chip)
                issue(level - 1, u)

            @pl.when(s == 0)
            def _():
                wait_sibling(u)

            for step in range(1, chips):
                wait_slot(level, u, (chip + step) % chips)
            fold(level, u)

            @pl.when(s == z)
            def _():
                finish(u)
        return carry

    lax.fori_loop(0, z + 1, one_level, 0)

    for u in range(units):
        for turn in range(2):
            @pl.when(z < levels - 1)
            def _():
                for one in first_up(u, turn):
                    one.wait_send()

            for one in first_copies(u, turn):
                one.wait_send()

    def drain(s, carry):
        level = z - s
        for u in range(units):
            @pl.when(z < levels - 1)
            def _():
                up(level, u).wait_send()

            for step in range(1, chips):
                across(level, u, step).wait_send()
        return carry

    lax.fori_loop(1, z + 1, drain, 0)
    swap.wait_send()
    for step in range(1, peers):
        gate_copy(step).wait_send()
    for u in range(units):
        out_own(u).wait()
        out_swap(u).wait_send()
        send(
            stage.at[u, 1 - core], out_lanes(1 - core, u),
            out_send.at[u], out_recv.at[u], {"head": sibling},
        ).wait_recv()


def body(levels, peers, q, k, v, frames, noise, mask, gate):
    rows, kv_width = k.shape
    kv_heads = kv_width // HD // CORES
    group_rows = q.shape[1] // kv_width * rows * CORES
    chips = peers // CORES
    units = kv_heads // 2
    level_spans = peers * rows // CT
    gate_rows = -(-(gate.shape[1] // HD) // 8) * 8
    hbm = pl.BlockSpec(memory_space=pltpu.HBM)
    pairs = q.shape[0] * q.shape[1] // HD * levels * peers * rows
    unit_width = kv_width // CORES // units
    out_width = q.shape[1] // CORES // units
    return pl.pallas_call(
        functools.partial(kernel, levels, peers, units),
        out_shape=jax.ShapeDtypeStruct(q.shape, q.dtype),
        in_specs=[hbm] * 7,
        out_specs=hbm,
        scratch_shapes=[
            pltpu.VMEM((levels, units, chips, 2, CORES, rows, unit_width), k.dtype),
            pltpu.VMEM((CORES, rows, q.shape[1] // CORES), q.dtype),
            pltpu.VMEM((units, CORES, rows, out_width), q.dtype),
            pltpu.VMEM(gate.shape, gate.dtype),
            pltpu.SMEM(frames.shape, frames.dtype),
            pltpu.SMEM(noise.shape, noise.dtype),
            pltpu.SMEM(mask.shape, mask.dtype),
            pltpu.VMEM((kv_heads, group_rows, 2 * HD), jnp.float32),
            pltpu.VMEM((kv_heads, group_rows, HD), jnp.float32),
            pltpu.VMEM((level_spans, gate_rows, HD), jnp.float32),
            pltpu.VMEM((peers, gate_rows, HD), jnp.float32),
            pltpu.SemaphoreType.DMA((levels, units, chips)),
            pltpu.SemaphoreType.DMA((units, 2, 2, chips + 1)),
            pltpu.SemaphoreType.DMA((levels, units)),
            pltpu.SemaphoreType.DMA((levels, units, max(chips - 1, 1))),
            pltpu.SemaphoreType.DMA((peers,)),
            pltpu.SemaphoreType.DMA((peers,)),
            pltpu.SemaphoreType.DMA((units, 2)),
            pltpu.SemaphoreType.DMA((5,)),
            pltpu.SemaphoreType.DMA((1,)),
            pltpu.SemaphoreType.DMA((1,)),
            pltpu.SemaphoreType.DMA((units,)),
            pltpu.SemaphoreType.DMA((units,)),
            pltpu.SemaphoreType.DMA((units,)),
        ],
        compiler_params=pltpu.CompilerParams(
            collective_id=0, has_side_effects=True, vmem_limit_bytes=64 << 20
        ),
        cost_estimate=pl.CostEstimate(
            flops=pairs * HD * 4, bytes_accessed=4 * q.size, transcendentals=pairs
        ),
    )(q, k, v, frames, noise, mask, gate)


def solution(mesh):
    placed = (
        P(("groups", "span", "head"), None),
        P(("groups", "span", "head"), None),
        P(("groups", "span", "head"), None),
        P("groups"),
        P("groups"),
        P("groups", None),
        P(None, "head"),
    )
    return jax.shard_map(
        functools.partial(body, mesh.shape["span"], mesh.shape["head"]),
        mesh=mesh,
        in_specs=placed,
        out_specs=P(("groups", "span", "head"), None),
        check_vma=False,
    )
```

```python
import functools
import math

import jax
import jax.numpy as jnp
from jax import lax
from jax.experimental import pallas as pl
from jax.experimental.pallas import tpu as pltpu
from jax.sharding import PartitionSpec as P

HD = 128
FRAME_TOK = 32
CT = 128
CORES = 2
MESH = pl.DeviceIdType.MESH
LOW = -1e30


def kernel(
    levels, peers, units,
    q_hbm, k_hbm, v_hbm, frames_hbm, noise_hbm, mask_hbm, gate_hbm,
    out_hbm,
    kv_buf, q_ref, stage, gate_ref, frames_ref, noise_ref, mask_ref, acc, top, gate_out, gate_in,
    recv_sem, first_sem, up_sem, across_sem, other_sem, gate_send, gate_recv, own_sem, load_sem,
    q_send, q_recv, out_send, out_recv, out_sem,
):
    rows, kv_width = k_hbm.shape
    kv_heads = kv_width // HD // CORES
    heads = q_hbm.shape[1] // HD // CORES
    group = heads // kv_heads
    heads_dev = gate_hbm.shape[1] // HD
    chips = peers // CORES
    chip_rows = CORES * rows
    level_rows = peers * rows
    level_spans = level_rows // CT
    unit_heads = kv_heads // units
    unit_width = unit_heads * HD
    factor = math.log2(math.e) / math.sqrt(HD)

    z = lax.axis_index("span")
    me = lax.axis_index("head")
    chip, core = me // CORES, me % CORES
    sibling = chip * CORES + (1 - core)

    barrier = pltpu.get_barrier_semaphore()
    for step in range(1, peers):
        pl.semaphore_signal(
            barrier, inc=1, device_id={"head": (me + step) % peers}, device_id_type=MESH
        )

    @pl.when(z > 0)
    def _():
        for other in (me, sibling):
            pl.semaphore_signal(
                barrier, inc=1, device_id={"span": z - 1, "head": other}, device_id_type=MESH
            )

    def lanes_of(owner, unit, width):
        start = (owner * units + unit) * width
        return pl.ds(pl.multiple_of(start, width), width)

    def piece(kv, owner, unit):
        return (k_hbm, v_hbm)[kv].at[:, lanes_of(owner, unit, unit_width)]

    def place(level, unit, slot, kv):
        return kv_buf.at[level, unit, slot, kv, core]

    def half(ref, owner):
        return ref.at[:, pl.ds(pl.multiple_of(owner * heads * HD, heads * HD), heads * HD)]

    loads = [
        pltpu.make_async_copy(source, target, load_sem.at[n])
        for n, (source, target) in enumerate(
            (
                (frames_hbm, frames_ref),
                (noise_hbm, noise_ref),
                (mask_hbm, mask_ref),
                (gate_hbm, gate_ref),
                (half(q_hbm, core), q_ref.at[core]),
            )
        )
    ]
    for load in loads:
        load.start()
    own = [
        pltpu.make_async_copy(piece(kv, core, u), place(z, u, chip, kv), own_sem.at[u, kv])
        for u in range(units)
        for kv in range(2)
    ]
    for load in own:
        load.start()

    pl.semaphore_wait(barrier, peers - 1 + jnp.where(z < levels - 1, CORES, 0))

    def send(source, target, send_sem, arrive_sem, device):
        return pltpu.make_async_remote_copy(
            src_ref=source,
            dst_ref=target,
            send_sem=send_sem,
            recv_sem=arrive_sem,
            device_id=device,
            device_id_type=MESH,
        )

    def first(unit, kv, turn, hop):
        owner = core if turn == 0 else 1 - core
        target = place(z, unit, chip, kv)
        if hop == "up":
            device = {"span": z + 1, "head": chip * CORES + owner}
            index = 0
        else:
            device = {"head": ((chip + hop) % chips) * CORES + owner}
            index = 1 + hop
        return send(
            piece(kv, owner, unit), target, first_sem.at[unit, kv, turn, index],
            recv_sem.at[z, unit, chip], device,
        )

    def first_copies(unit, turn):
        hops = list(range(1, chips)) + ([0] if turn else [])
        return [first(unit, kv, turn, hop) for hop in hops for kv in range(2)]

    def first_up(unit, turn):
        return [first(unit, kv, turn, "up") for kv in range(2)]

    def up(level, unit):
        slot = kv_buf.at[level, unit, chip]
        return send(
            slot, slot, up_sem.at[level, unit], recv_sem.at[level, unit, chip], {"span": z + 1}
        )

    def across(level, unit, step):
        slot = kv_buf.at[level, unit, chip]
        return send(
            slot, slot, across_sem.at[level, unit, step - 1], recv_sem.at[level, unit, chip],
            {"head": ((chip + step) % chips) * CORES + core},
        )

    def wait_slot(level, unit, slot):
        whole = kv_buf.at[level, unit, slot]
        send(
            whole, whole, up_sem.at[level, unit], recv_sem.at[level, unit, slot],
            {"head": sibling},
        ).wait_recv()

    def wait_sibling(unit):
        rest = kv_buf.at[z, unit, chip, :, 1 - core]
        send(
            rest, rest, up_sem.at[z, unit], recv_sem.at[z, unit, chip], {"head": sibling}
        ).wait_recv()

    def by_span(unit):
        return chips == 2 and unit % 2 == 1

    def up_other(unit, step):
        slot = kv_buf.at[0, unit, (chip + step) % chips]
        return send(
            slot, slot, other_sem.at[unit, step - 1],
            recv_sem.at[0, unit, (chip + step) % chips], {"span": z + 1},
        )

    def goes_across(level, unit):
        return (level > 0) if by_span(unit) else (level >= 0)

    def issue(level, unit):
        @pl.when(z < levels - 1)
        def _():
            up(level, unit).start()

        @pl.when(goes_across(level, unit))
        def _():
            for step in range(1, chips):
                across(level, unit, step).start()

    swap = send(
        half(q_hbm, 1 - core), q_ref.at[core], q_send.at[0], q_recv.at[0], {"head": sibling}
    )

    def gate_copy(step):
        target = (me + step) % peers
        return send(
            gate_out.at[(target * rows) // CT], gate_in.at[me],
            gate_send.at[step], gate_recv.at[me], {"head": target},
        )

    for u in range(units):
        for turn in range(2):
            @pl.when(z < levels - 1)
            def _():
                for one in first_up(u, turn):
                    one.start()

            for one in first_copies(u, turn):
                one.start()
        if u == 0:
            swap.start()

    acc[...] = jnp.zeros_like(acc)
    top[...] = jnp.full_like(top, LOW)
    for load in loads:
        load.wait()
    for i in range(level_spans):
        level_index = noise_ref[z * level_spans + i]
        pick = lax.broadcasted_iota(jnp.int32, (8, gate_ref.shape[0]), 1) == level_index
        picked = jnp.dot(
            pick.astype(jnp.bfloat16), gate_ref[...], preferred_element_type=jnp.float32
        )
        for n in range(heads_dev):
            gate_out[i, n : n + 1, :] = picked[0:1, n * HD : (n + 1) * HD]
    for step in range(1, peers):
        gate_copy(step).start()

    token = chip * chip_rows
    span = z * level_spans + token // CT
    gate_in[me] = gate_out[token // CT]
    for load in own:
        load.wait()
    send(
        q_ref.at[1 - core], q_ref.at[1 - core], q_send.at[0], q_recv.at[0], {"head": sibling}
    ).wait_recv()
    for step in range(1, peers):
        source = (me + step) % peers
        send(
            gate_out.at[0], gate_in.at[source], gate_send.at[step], gate_recv.at[source],
            {"head": source},
        ).wait_recv()

    def fold(level, unit):
        column = lax.broadcasted_iota(jnp.int32, (1, level_rows), 1)
        usable = column < 0
        for i in range(level_spans):
            key_span = level * level_spans + i
            limit = jnp.where(mask_ref[span, key_span] > 0, frames_ref[key_span] * FRAME_TOK, 0)
            usable = usable | ((column >= i * CT) & (column < i * CT + limit))
        bias = jnp.where(usable, jnp.float32(0.0), jnp.float32(LOW))
        ones = jnp.ones((level_rows, HD), jnp.bfloat16)

        for n in range(unit_heads):
            j = unit * unit_heads + n
            lanes = slice(n * HD, (n + 1) * HD)
            queries = jnp.concatenate(
                [
                    q_ref[:, :, (j * group + g) * HD : (j * group + g + 1) * HD].reshape(
                        chip_rows, HD
                    )
                    for g in range(group)
                ],
                axis=0,
            )
            keys = kv_buf[level, unit, :, 0, :, :, lanes].reshape(level_rows, HD)
            values = kv_buf[level, unit, :, 1, :, :, lanes].reshape(level_rows, HD)
            scores = lax.dot_general(
                queries, keys, (((1,), (1,)), ((), ())), preferred_element_type=jnp.float32
            )
            scores = scores + bias
            old = top[j]
            new = jnp.maximum(old, jnp.max(scores, axis=1, keepdims=True))
            top[j] = new
            wide = jnp.concatenate([new] * (level_rows // HD), axis=1)
            weights = jnp.exp2((scores - wide) * factor).astype(jnp.bfloat16)
            update = jnp.dot(
                weights,
                jnp.concatenate([values, ones], axis=1),
                preferred_element_type=jnp.float32,
            )
            shrink = jnp.exp2((old - new) * factor)
            acc[j] = acc[j] * jnp.concatenate([shrink, shrink], axis=1) + update

    position = token % CT + lax.broadcasted_iota(jnp.int32, (chip_rows, HD), 0)
    live = position < frames_ref[span] * FRAME_TOK
    out_width = unit_width * group

    def out_lanes(owner, unit):
        return out_hbm.at[:, lanes_of(owner, unit, out_width)]

    def out_own(unit):
        return pltpu.make_async_copy(
            stage.at[unit, core], out_lanes(core, unit), out_sem.at[unit]
        )

    def out_swap(unit):
        return send(
            stage.at[unit, 1 - core], out_lanes(core, unit),
            out_send.at[unit], out_recv.at[unit], {"head": sibling},
        )

    def finish(unit):
        for n in range(unit_heads):
            j = unit * unit_heads + n
            for g in range(group):
                head = j * group + g
                part = slice(g * chip_rows, (g + 1) * chip_rows)
                row = head % heads_dev
                gate = gate_in[core * (peers // CORES) + head // heads_dev, row : row + 1, :]
                ratio = acc[j, part, :HD] / acc[j, part, HD:]
                done = jnp.where(live, ratio * gate, jnp.float32(0.0)).astype(stage.dtype)
                at = slice((n * group + g) * HD, (n * group + g + 1) * HD)
                stage[unit, :, :, at] = done.reshape(CORES, rows, HD)
        out_swap(unit).start()
        out_own(unit).start()

    def one_level(s, carry):
        level = z - s
        for u in range(units):
            @pl.when(s < z)
            def _():
                wait_slot(level - 1, u, chip)
                issue(level - 1, u)

            @pl.when(s == 0)
            def _():
                wait_sibling(u)

            for step in range(1, chips):
                wait_slot(level, u, (chip + step) % chips)
            if by_span(u):
                @pl.when((s == z) & (z < levels - 1))
                def _():
                    for step in range(1, chips):
                        up_other(u, step).start()
            fold(level, u)

            @pl.when(s == z)
            def _():
                finish(u)
        return carry

    lax.fori_loop(0, z + 1, one_level, 0)

    for u in range(units):
        for turn in range(2):
            @pl.when(z < levels - 1)
            def _():
                for one in first_up(u, turn):
                    one.wait_send()

            for one in first_copies(u, turn):
                one.wait_send()

    def drain(s, carry):
        level = z - s
        for u in range(units):
            @pl.when(z < levels - 1)
            def _():
                up(level, u).wait_send()

            @pl.when(goes_across(level, u))
            def _():
                for step in range(1, chips):
                    across(level, u, step).wait_send()
        return carry

    lax.fori_loop(1, z + 1, drain, 0)
    for u in range(units):
        if by_span(u):
            @pl.when(z < levels - 1)
            def _():
                for step in range(1, chips):
                    up_other(u, step).wait_send()
    swap.wait_send()
    for step in range(1, peers):
        gate_copy(step).wait_send()
    for u in range(units):
        out_own(u).wait()
        out_swap(u).wait_send()
        send(
            stage.at[u, 1 - core], out_lanes(1 - core, u),
            out_send.at[u], out_recv.at[u], {"head": sibling},
        ).wait_recv()


def body(levels, peers, q, k, v, frames, noise, mask, gate):
    rows, kv_width = k.shape
    kv_heads = kv_width // HD // CORES
    group_rows = q.shape[1] // kv_width * rows * CORES
    chips = peers // CORES
    units = kv_heads // 2
    level_spans = peers * rows // CT
    gate_rows = -(-(gate.shape[1] // HD) // 8) * 8
    hbm = pl.BlockSpec(memory_space=pltpu.HBM)
    pairs = q.shape[0] * q.shape[1] // HD * levels * peers * rows
    unit_width = kv_width // CORES // units
    out_width = q.shape[1] // CORES // units
    return pl.pallas_call(
        functools.partial(kernel, levels, peers, units),
        out_shape=jax.ShapeDtypeStruct(q.shape, q.dtype),
        in_specs=[hbm] * 7,
        out_specs=pl.BlockSpec(memory_space=pltpu.VMEM),
        scratch_shapes=[
            pltpu.VMEM((levels, units, chips, 2, CORES, rows, unit_width), k.dtype),
            pltpu.VMEM((CORES, rows, q.shape[1] // CORES), q.dtype),
            pltpu.VMEM((units, CORES, rows, out_width), q.dtype),
            pltpu.VMEM(gate.shape, gate.dtype),
            pltpu.SMEM(frames.shape, frames.dtype),
            pltpu.SMEM(noise.shape, noise.dtype),
            pltpu.SMEM(mask.shape, mask.dtype),
            pltpu.VMEM((kv_heads, group_rows, 2 * HD), jnp.float32),
            pltpu.VMEM((kv_heads, group_rows, HD), jnp.float32),
            pltpu.VMEM((level_spans, gate_rows, HD), jnp.float32),
            pltpu.VMEM((peers, gate_rows, HD), jnp.float32),
            pltpu.SemaphoreType.DMA((levels, units, chips)),
            pltpu.SemaphoreType.DMA((units, 2, 2, chips + 1)),
            pltpu.SemaphoreType.DMA((levels, units)),
            pltpu.SemaphoreType.DMA((levels, units, max(chips - 1, 1))),
            pltpu.SemaphoreType.DMA((units, max(chips - 1, 1))),
            pltpu.SemaphoreType.DMA((peers,)),
            pltpu.SemaphoreType.DMA((peers,)),
            pltpu.SemaphoreType.DMA((units, 2)),
            pltpu.SemaphoreType.DMA((5,)),
            pltpu.SemaphoreType.DMA((1,)),
            pltpu.SemaphoreType.DMA((1,)),
            pltpu.SemaphoreType.DMA((units,)),
            pltpu.SemaphoreType.DMA((units,)),
            pltpu.SemaphoreType.DMA((units,)),
        ],
        compiler_params=pltpu.CompilerParams(
            collective_id=0, has_side_effects=True, vmem_limit_bytes=48 << 20
        ),
        cost_estimate=pl.CostEstimate(
            flops=pairs * HD * 4, bytes_accessed=4 * q.size, transcendentals=pairs
        ),
    )(*[pltpu.with_memory_space_constraint(x, pltpu.HBM) for x in (q, k, v, frames, noise, mask, gate)])


def solution(mesh):
    placed = (
        P(("groups", "span", "head"), None),
        P(("groups", "span", "head"), None),
        P(("groups", "span", "head"), None),
        P("groups"),
        P("groups"),
        P("groups", None),
        P(None, "head"),
    )
    return jax.shard_map(
        functools.partial(body, mesh.shape["span"], mesh.shape["head"]),
        mesh=mesh,
        in_specs=placed,
        out_specs=P(("groups", "span", "head"), None),
        check_vma=False,
    )
```

```python
import functools
import math

import jax
import jax.numpy as jnp
from jax import lax
from jax.experimental import pallas as pl
from jax.experimental.pallas import tpu as pltpu
from jax.sharding import PartitionSpec as P

HD = 128
FRAME_TOK = 32
CT = 128
CORES = 2
MESH = pl.DeviceIdType.MESH
LOW = -1e30


def kernel(
    levels, peers, units,
    q_hbm, k_hbm, v_hbm, frames_hbm, noise_hbm, mask_hbm, gate_hbm,
    out_hbm,
    kv_buf, q_ref, stage, gate_ref, frames_ref, noise_ref, mask_ref, acc, top, gate_out, gate_in,
    recv_sem, first_sem, up_sem, across_sem, other_sem, gate_send, gate_recv, own_sem, load_sem,
    q_send, q_recv, out_send, out_recv, out_sem,
):
    rows, kv_width = k_hbm.shape
    kv_heads = kv_width // HD // CORES
    heads = q_hbm.shape[1] // HD // CORES
    group = heads // kv_heads
    heads_dev = gate_hbm.shape[1] // HD
    chips = peers // CORES
    chip_rows = CORES * rows
    level_rows = peers * rows
    level_spans = level_rows // CT
    unit_heads = kv_heads // units
    unit_width = unit_heads * HD
    factor = math.log2(math.e) / math.sqrt(HD)

    z = lax.axis_index("span")
    me = lax.axis_index("head")
    chip, core = me // CORES, me % CORES
    sibling = chip * CORES + (1 - core)

    barrier = pltpu.get_barrier_semaphore()
    for step in range(1, peers):
        pl.semaphore_signal(
            barrier, inc=1, device_id={"head": (me + step) % peers}, device_id_type=MESH
        )

    @pl.when(z > 0)
    def _():
        for other in (me, sibling):
            pl.semaphore_signal(
                barrier, inc=1, device_id={"span": z - 1, "head": other}, device_id_type=MESH
            )

    def lanes_of(owner, unit, width):
        start = (owner * units + unit) * width
        return pl.ds(pl.multiple_of(start, width), width)

    def piece(kv, owner, unit):
        return (k_hbm, v_hbm)[kv].at[:, lanes_of(owner, unit, unit_width)]

    def place(level, unit, slot, kv):
        return kv_buf.at[level, unit, slot, kv, core]

    def half(ref, owner):
        return ref.at[:, pl.ds(pl.multiple_of(owner * heads * HD, heads * HD), heads * HD)]

    loads = [
        pltpu.make_async_copy(source, target, load_sem.at[n])
        for n, (source, target) in enumerate(
            (
                (frames_hbm, frames_ref),
                (noise_hbm, noise_ref),
                (mask_hbm, mask_ref),
                (gate_hbm, gate_ref),
                (half(q_hbm, core), q_ref.at[core]),
            )
        )
    ]
    for load in loads:
        load.start()
    own = [
        pltpu.make_async_copy(piece(kv, core, u), place(z, u, chip, kv), own_sem.at[u, kv])
        for u in range(units)
        for kv in range(2)
    ]
    for load in own:
        load.start()

    pl.semaphore_wait(barrier, peers - 1 + jnp.where(z < levels - 1, CORES, 0))

    def send(source, target, send_sem, arrive_sem, device):
        return pltpu.make_async_remote_copy(
            src_ref=source,
            dst_ref=target,
            send_sem=send_sem,
            recv_sem=arrive_sem,
            device_id=device,
            device_id_type=MESH,
        )

    def first(unit, kv, turn, hop):
        owner = core if turn == 0 else 1 - core
        target = place(z, unit, chip, kv)
        if hop == "up":
            device = {"span": z + 1, "head": chip * CORES + owner}
            index = 0
        else:
            device = {"head": ((chip + hop) % chips) * CORES + owner}
            index = 1 + hop
        return send(
            piece(kv, owner, unit), target, first_sem.at[unit, kv, turn, index],
            recv_sem.at[z, unit, chip], device,
        )

    def first_copies(unit, turn):
        hops = list(range(1, chips)) + ([0] if turn else [])
        return [first(unit, kv, turn, hop) for hop in hops for kv in range(2)]

    def first_up(unit, turn):
        return [first(unit, kv, turn, "up") for kv in range(2)]

    def up(level, unit):
        slot = kv_buf.at[level, unit, chip]
        return send(
            slot, slot, up_sem.at[level, unit], recv_sem.at[level, unit, chip], {"span": z + 1}
        )

    def across(level, unit, step):
        slot = kv_buf.at[level, unit, chip]
        return send(
            slot, slot, across_sem.at[level, unit, step - 1], recv_sem.at[level, unit, chip],
            {"head": ((chip + step) % chips) * CORES + core},
        )

    def wait_slot(level, unit, slot):
        whole = kv_buf.at[level, unit, slot]
        send(
            whole, whole, up_sem.at[level, unit], recv_sem.at[level, unit, slot],
            {"head": sibling},
        ).wait_recv()

    def wait_sibling(unit):
        rest = kv_buf.at[z, unit, chip, :, 1 - core]
        send(
            rest, rest, up_sem.at[z, unit], recv_sem.at[z, unit, chip], {"head": sibling}
        ).wait_recv()

    def by_span(unit):
        return chips == 2 and unit % 2 == 1

    def up_other(unit, step):
        slot = kv_buf.at[0, unit, (chip + step) % chips]
        return send(
            slot, slot, other_sem.at[unit, step - 1],
            recv_sem.at[0, unit, (chip + step) % chips], {"span": z + 1},
        )

    def goes_across(level, unit):
        return (level > 0) if by_span(unit) else (level >= 0)

    def issue(level, unit):
        @pl.when(z < levels - 1)
        def _():
            up(level, unit).start()

        @pl.when(goes_across(level, unit))
        def _():
            for step in range(1, chips):
                across(level, unit, step).start()

    swap = send(
        half(q_hbm, 1 - core), q_ref.at[core], q_send.at[0], q_recv.at[0], {"head": sibling}
    )

    def gate_copy(step):
        target = (me + step) % peers
        return send(
            gate_out.at[(target * rows) // CT], gate_in.at[me],
            gate_send.at[step], gate_recv.at[me], {"head": target},
        )

    for u in range(units):
        for turn in range(2):
            @pl.when(z < levels - 1)
            def _():
                for one in first_up(u, turn):
                    one.start()

            for one in first_copies(u, turn):
                one.start()
        if u == 0:
            swap.start()

    acc[...] = jnp.zeros_like(acc)
    top[...] = jnp.full_like(top, LOW)
    for load in loads:
        load.wait()
    for i in range(level_spans):
        level_index = noise_ref[z * level_spans + i]
        pick = lax.broadcasted_iota(jnp.int32, (8, gate_ref.shape[0]), 1) == level_index
        picked = jnp.dot(
            pick.astype(jnp.bfloat16), gate_ref[...], preferred_element_type=jnp.float32
        )
        for n in range(heads_dev):
            gate_out[i, n : n + 1, :] = picked[0:1, n * HD : (n + 1) * HD]
    for step in range(1, peers):
        gate_copy(step).start()

    token = chip * chip_rows
    span = z * level_spans + token // CT
    gate_in[me] = gate_out[token // CT]
    for load in own:
        load.wait()
    send(
        q_ref.at[1 - core], q_ref.at[1 - core], q_send.at[0], q_recv.at[0], {"head": sibling}
    ).wait_recv()
    for step in range(1, peers):
        source = (me + step) % peers
        send(
            gate_out.at[0], gate_in.at[source], gate_send.at[step], gate_recv.at[source],
            {"head": source},
        ).wait_recv()

    def fold(level, unit):
        column = lax.broadcasted_iota(jnp.int32, (1, level_rows), 1)
        usable = column < 0
        for i in range(level_spans):
            key_span = level * level_spans + i
            limit = jnp.where(mask_ref[span, key_span] > 0, frames_ref[key_span] * FRAME_TOK, 0)
            usable = usable | ((column >= i * CT) & (column < i * CT + limit))
        bias = jnp.where(usable, jnp.float32(0.0), jnp.float32(LOW))
        ones = jnp.ones((level_rows, HD), jnp.bfloat16)

        for n in range(unit_heads):
            j = unit * unit_heads + n
            lanes = slice(n * HD, (n + 1) * HD)
            queries = jnp.concatenate(
                [
                    q_ref[:, :, (j * group + g) * HD : (j * group + g + 1) * HD].reshape(
                        chip_rows, HD
                    )
                    for g in range(group)
                ],
                axis=0,
            )
            keys = kv_buf[level, unit, :, 0, :, :, lanes].reshape(level_rows, HD)
            values = kv_buf[level, unit, :, 1, :, :, lanes].reshape(level_rows, HD)
            scores = lax.dot_general(
                queries, keys, (((1,), (1,)), ((), ())), preferred_element_type=jnp.float32
            )
            scores = scores + bias
            old = top[j]
            new = jnp.maximum(old, jnp.max(scores, axis=1, keepdims=True))
            top[j] = new
            wide = jnp.concatenate([new] * (level_rows // HD), axis=1)
            weights = jnp.exp2((scores - wide) * factor).astype(jnp.bfloat16)
            update = jnp.dot(
                weights,
                jnp.concatenate([values, ones], axis=1),
                preferred_element_type=jnp.float32,
            )
            shrink = jnp.exp2((old - new) * factor)
            acc[j] = acc[j] * jnp.concatenate([shrink, shrink], axis=1) + update

    position = token % CT + lax.broadcasted_iota(jnp.int32, (chip_rows, HD), 0)
    live = position < frames_ref[span] * FRAME_TOK
    out_width = unit_width * group

    def out_lanes(owner, unit):
        return out_hbm.at[:, lanes_of(owner, unit, out_width)]

    def out_own(unit):
        return pltpu.make_async_copy(
            stage.at[unit, core], out_lanes(core, unit), out_sem.at[unit]
        )

    def out_swap(unit):
        return send(
            stage.at[unit, 1 - core], out_lanes(core, unit),
            out_send.at[unit], out_recv.at[unit], {"head": sibling},
        )

    def finish(unit):
        for n in range(unit_heads):
            j = unit * unit_heads + n
            for g in range(group):
                head = j * group + g
                part = slice(g * chip_rows, (g + 1) * chip_rows)
                row = head % heads_dev
                gate = gate_in[core * (peers // CORES) + head // heads_dev, row : row + 1, :]
                ratio = acc[j, part, :HD] / acc[j, part, HD:]
                done = jnp.where(live, ratio * gate, jnp.float32(0.0)).astype(stage.dtype)
                at = slice((n * group + g) * HD, (n * group + g + 1) * HD)
                stage[unit, :, :, at] = done.reshape(CORES, rows, HD)
        out_swap(unit).start()
        out_own(unit).start()

    def one_level(s, carry):
        level = z - s
        for u in range(units):
            @pl.when(s < z)
            def _():
                wait_slot(level - 1, u, chip)
                issue(level - 1, u)

            @pl.when(s == 0)
            def _():
                wait_sibling(u)

            for step in range(1, chips):
                wait_slot(level, u, (chip + step) % chips)
            if by_span(u):
                @pl.when((s == z) & (z < levels - 1))
                def _():
                    for step in range(1, chips):
                        up_other(u, step).start()
            fold(level, u)

            @pl.when(s == z)
            def _():
                finish(u)
        return carry

    lax.fori_loop(0, z + 1, one_level, 0)

    for u in range(units):
        for turn in range(2):
            @pl.when(z < levels - 1)
            def _():
                for one in first_up(u, turn):
                    one.wait_send()

            for one in first_copies(u, turn):
                one.wait_send()

    def drain(s, carry):
        level = z - s
        for u in range(units):
            @pl.when(z < levels - 1)
            def _():
                up(level, u).wait_send()

            @pl.when(goes_across(level, u))
            def _():
                for step in range(1, chips):
                    across(level, u, step).wait_send()
        return carry

    lax.fori_loop(1, z + 1, drain, 0)
    for u in range(units):
        if by_span(u):
            @pl.when(z < levels - 1)
            def _():
                for step in range(1, chips):
                    up_other(u, step).wait_send()
    swap.wait_send()
    for step in range(1, peers):
        gate_copy(step).wait_send()
    for u in range(units):
        out_own(u).wait()
        out_swap(u).wait_send()
        send(
            stage.at[u, 1 - core], out_lanes(1 - core, u),
            out_send.at[u], out_recv.at[u], {"head": sibling},
        ).wait_recv()


def body(levels, peers, q, k, v, frames, noise, mask, gate):
    rows, kv_width = k.shape
    kv_heads = kv_width // HD // CORES
    group_rows = q.shape[1] // kv_width * rows * CORES
    chips = peers // CORES
    units = kv_heads
    level_spans = peers * rows // CT
    gate_rows = -(-(gate.shape[1] // HD) // 8) * 8
    hbm = pl.BlockSpec(memory_space=pltpu.HBM)
    pairs = q.shape[0] * q.shape[1] // HD * levels * peers * rows
    unit_width = kv_width // CORES // units
    out_width = q.shape[1] // CORES // units
    return pl.pallas_call(
        functools.partial(kernel, levels, peers, units),
        out_shape=jax.ShapeDtypeStruct(q.shape, q.dtype),
        in_specs=[hbm] * 7,
        out_specs=pl.BlockSpec(memory_space=pltpu.VMEM),
        scratch_shapes=[
            pltpu.VMEM((levels, units, chips, 2, CORES, rows, unit_width), k.dtype),
            pltpu.VMEM((CORES, rows, q.shape[1] // CORES), q.dtype),
            pltpu.VMEM((units, CORES, rows, out_width), q.dtype),
            pltpu.VMEM(gate.shape, gate.dtype),
            pltpu.SMEM(frames.shape, frames.dtype),
            pltpu.SMEM(noise.shape, noise.dtype),
            pltpu.SMEM(mask.shape, mask.dtype),
            pltpu.VMEM((kv_heads, group_rows, 2 * HD), jnp.float32),
            pltpu.VMEM((kv_heads, group_rows, HD), jnp.float32),
            pltpu.VMEM((level_spans, gate_rows, HD), jnp.float32),
            pltpu.VMEM((peers, gate_rows, HD), jnp.float32),
            pltpu.SemaphoreType.DMA((levels, units, chips)),
            pltpu.SemaphoreType.DMA((units, 2, 2, chips + 1)),
            pltpu.SemaphoreType.DMA((levels, units)),
            pltpu.SemaphoreType.DMA((levels, units, max(chips - 1, 1))),
            pltpu.SemaphoreType.DMA((units, max(chips - 1, 1))),
            pltpu.SemaphoreType.DMA((peers,)),
            pltpu.SemaphoreType.DMA((peers,)),
            pltpu.SemaphoreType.DMA((units, 2)),
            pltpu.SemaphoreType.DMA((5,)),
            pltpu.SemaphoreType.DMA((1,)),
            pltpu.SemaphoreType.DMA((1,)),
            pltpu.SemaphoreType.DMA((units,)),
            pltpu.SemaphoreType.DMA((units,)),
            pltpu.SemaphoreType.DMA((units,)),
        ],
        compiler_params=pltpu.CompilerParams(
            collective_id=0, has_side_effects=True, vmem_limit_bytes=48 << 20
        ),
        cost_estimate=pl.CostEstimate(
            flops=pairs * HD * 4, bytes_accessed=4 * q.size, transcendentals=pairs
        ),
    )(*[pltpu.with_memory_space_constraint(x, pltpu.HBM) for x in (q, k, v, frames, noise, mask, gate)])


def solution(mesh):
    placed = (
        P(("groups", "span", "head"), None),
        P(("groups", "span", "head"), None),
        P(("groups", "span", "head"), None),
        P("groups"),
        P("groups"),
        P("groups", None),
        P(None, "head"),
    )
    return jax.shard_map(
        functools.partial(body, mesh.shape["span"], mesh.shape["head"]),
        mesh=mesh,
        in_specs=placed,
        out_specs=P(("groups", "span", "head"), None),
        check_vma=False,
    )
```

```python
import functools
import math

import jax
import jax.numpy as jnp
from jax import lax
from jax.experimental import pallas as pl
from jax.experimental.pallas import tpu as pltpu
from jax.sharding import PartitionSpec as P

HD = 128
FRAME_TOK = 32
CT = 128
CORES = 2
FLIGHT = 2
MESH = pl.DeviceIdType.MESH
LOW = -1e30


def kernel(
    levels, peers, units,
    q_hbm, k_hbm, v_hbm, frames_hbm, noise_hbm, mask_hbm, gate_hbm,
    out_hbm,
    kv_buf, q_ref, stage, gate_ref, frames_ref, noise_ref, mask_ref, acc, top, gate_out, gate_in,
    recv_sem, first_sem, up_sem, across_sem, other_sem, gate_send, gate_recv, own_sem, load_sem,
    q_send, q_recv, out_send, out_recv, out_sem,
):
    rows, kv_width = k_hbm.shape
    kv_heads = kv_width // HD // CORES
    heads = q_hbm.shape[1] // HD // CORES
    group = heads // kv_heads
    heads_dev = gate_hbm.shape[1] // HD
    chips = peers // CORES
    chip_rows = CORES * rows
    level_rows = peers * rows
    level_spans = level_rows // CT
    unit_heads = kv_heads // units
    unit_width = unit_heads * HD
    factor = math.log2(math.e) / math.sqrt(HD)

    z = lax.axis_index("span")
    me = lax.axis_index("head")
    chip, core = me // CORES, me % CORES
    sibling = chip * CORES + (1 - core)

    barrier = pltpu.get_barrier_semaphore()
    for step in range(1, peers):
        pl.semaphore_signal(
            barrier, inc=1, device_id={"head": (me + step) % peers}, device_id_type=MESH
        )

    @pl.when(z > 0)
    def _():
        for other in (me, sibling):
            pl.semaphore_signal(
                barrier, inc=1, device_id={"span": z - 1, "head": other}, device_id_type=MESH
            )

    def lanes_of(owner, unit, width):
        start = (owner * units + unit) * width
        return pl.ds(pl.multiple_of(start, width), width)

    def piece(kv, owner, unit):
        return (k_hbm, v_hbm)[kv].at[:, lanes_of(owner, unit, unit_width)]

    def place(level, unit, slot, kv):
        return kv_buf.at[level, unit, slot, kv, core]

    def half(ref, owner):
        return ref.at[:, pl.ds(pl.multiple_of(owner * heads * HD, heads * HD), heads * HD)]

    loads = [
        pltpu.make_async_copy(source, target, load_sem.at[n])
        for n, (source, target) in enumerate(
            (
                (frames_hbm, frames_ref),
                (noise_hbm, noise_ref),
                (mask_hbm, mask_ref),
                (gate_hbm, gate_ref),
                (half(q_hbm, core), q_ref.at[core]),
            )
        )
    ]
    for load in loads:
        load.start()
    own = [
        pltpu.make_async_copy(piece(kv, core, u), place(z, u, chip, kv), own_sem.at[u, kv])
        for u in range(units)
        for kv in range(2)
    ]
    for load in own:
        load.start()

    pl.semaphore_wait(barrier, peers - 1 + jnp.where(z < levels - 1, CORES, 0))

    def send(source, target, send_sem, arrive_sem, device):
        return pltpu.make_async_remote_copy(
            src_ref=source,
            dst_ref=target,
            send_sem=send_sem,
            recv_sem=arrive_sem,
            device_id=device,
            device_id_type=MESH,
        )

    def first(unit, kv, turn, hop):
        owner = core if turn == 0 else 1 - core
        target = place(z, unit, chip, kv)
        if hop == "up":
            device = {"span": z + 1, "head": chip * CORES + owner}
            index = 0
        else:
            device = {"head": ((chip + hop) % chips) * CORES + owner}
            index = 1 + hop
        return send(
            piece(kv, owner, unit), target, first_sem.at[unit, kv, turn, index],
            recv_sem.at[z, unit, chip], device,
        )

    def first_copies(unit, turn):
        hops = list(range(1, chips)) + ([0] if turn else [])
        return [first(unit, kv, turn, hop) for hop in hops for kv in range(2)]

    def first_up(unit, turn):
        return [first(unit, kv, turn, "up") for kv in range(2)]

    def up(level, unit):
        slot = kv_buf.at[level, unit, chip]
        return send(
            slot, slot, up_sem.at[level, unit], recv_sem.at[level, unit, chip], {"span": z + 1}
        )

    def across(level, unit, step):
        slot = kv_buf.at[level, unit, chip]
        return send(
            slot, slot, across_sem.at[level, unit, step - 1], recv_sem.at[level, unit, chip],
            {"head": ((chip + step) % chips) * CORES + core},
        )

    def wait_slot(level, unit, slot):
        whole = kv_buf.at[level, unit, slot]
        send(
            whole, whole, up_sem.at[level, unit], recv_sem.at[level, unit, slot],
            {"head": sibling},
        ).wait_recv()

    def wait_sibling(unit):
        rest = kv_buf.at[z, unit, chip, :, 1 - core]
        send(
            rest, rest, up_sem.at[z, unit], recv_sem.at[z, unit, chip], {"head": sibling}
        ).wait_recv()

    def by_span(unit):
        return chips == 2 and unit % 2 == 1

    def up_other(unit, step):
        slot = kv_buf.at[0, unit, (chip + step) % chips]
        return send(
            slot, slot, other_sem.at[unit, step - 1],
            recv_sem.at[0, unit, (chip + step) % chips], {"span": z + 1},
        )

    def goes_across(level, unit):
        return (level > 0) if by_span(unit) else (level >= 0)

    def issue(level, unit):
        @pl.when(z < levels - 1)
        def _():
            up(level, unit).start()

        @pl.when(goes_across(level, unit))
        def _():
            for step in range(1, chips):
                across(level, unit, step).start()

    swap = send(
        half(q_hbm, 1 - core), q_ref.at[core], q_send.at[0], q_recv.at[0], {"head": sibling}
    )

    def gate_copy(step):
        target = (me + step) % peers
        return send(
            gate_out.at[(target * rows) // CT], gate_in.at[me],
            gate_send.at[step], gate_recv.at[me], {"head": target},
        )

    def first_hop(unit, action):
        for turn in range(2):
            @pl.when(z < levels - 1)
            def _():
                for one in first_up(unit, turn):
                    action(one)

            for one in first_copies(unit, turn):
                action(one)

    for u in range(min(FLIGHT, units)):
        first_hop(u, lambda one: one.start())
    swap.start()

    acc[...] = jnp.zeros_like(acc)
    top[...] = jnp.full_like(top, LOW)
    for load in loads:
        load.wait()
    for i in range(level_spans):
        level_index = noise_ref[z * level_spans + i]
        pick = lax.broadcasted_iota(jnp.int32, (8, gate_ref.shape[0]), 1) == level_index
        picked = jnp.dot(
            pick.astype(jnp.bfloat16), gate_ref[...], preferred_element_type=jnp.float32
        )
        for n in range(heads_dev):
            gate_out[i, n : n + 1, :] = picked[0:1, n * HD : (n + 1) * HD]
    for step in range(1, peers):
        gate_copy(step).start()

    token = chip * chip_rows
    span = z * level_spans + token // CT
    gate_in[me] = gate_out[token // CT]
    for u in range(FLIGHT, units):
        first_hop(u - FLIGHT, lambda one: one.wait_send())
        first_hop(u, lambda one: one.start())
    for load in own:
        load.wait()
    send(
        q_ref.at[1 - core], q_ref.at[1 - core], q_send.at[0], q_recv.at[0], {"head": sibling}
    ).wait_recv()
    for step in range(1, peers):
        source = (me + step) % peers
        send(
            gate_out.at[0], gate_in.at[source], gate_send.at[step], gate_recv.at[source],
            {"head": source},
        ).wait_recv()

    def fold(level, unit):
        column = lax.broadcasted_iota(jnp.int32, (1, level_rows), 1)
        usable = column < 0
        for i in range(level_spans):
            key_span = level * level_spans + i
            limit = jnp.where(mask_ref[span, key_span] > 0, frames_ref[key_span] * FRAME_TOK, 0)
            usable = usable | ((column >= i * CT) & (column < i * CT + limit))
        bias = jnp.where(usable, jnp.float32(0.0), jnp.float32(LOW))
        ones = jnp.ones((level_rows, HD), jnp.bfloat16)

        for n in range(unit_heads):
            j = unit * unit_heads + n
            lanes = slice(n * HD, (n + 1) * HD)
            queries = jnp.concatenate(
                [
                    q_ref[:, :, (j * group + g) * HD : (j * group + g + 1) * HD].reshape(
                        chip_rows, HD
                    )
                    for g in range(group)
                ],
                axis=0,
            )
            keys = kv_buf[level, unit, :, 0, :, :, lanes].reshape(level_rows, HD)
            values = kv_buf[level, unit, :, 1, :, :, lanes].reshape(level_rows, HD)
            scores = lax.dot_general(
                queries, keys, (((1,), (1,)), ((), ())), preferred_element_type=jnp.float32
            )
            scores = scores + bias
            old = top[j]
            new = jnp.maximum(old, jnp.max(scores, axis=1, keepdims=True))
            top[j] = new
            wide = jnp.concatenate([new] * (level_rows // HD), axis=1)
            weights = jnp.exp2((scores - wide) * factor).astype(jnp.bfloat16)
            update = jnp.dot(
                weights,
                jnp.concatenate([values, ones], axis=1),
                preferred_element_type=jnp.float32,
            )
            shrink = jnp.exp2((old - new) * factor)
            acc[j] = acc[j] * jnp.concatenate([shrink, shrink], axis=1) + update

    position = token % CT + lax.broadcasted_iota(jnp.int32, (chip_rows, HD), 0)
    live = position < frames_ref[span] * FRAME_TOK
    out_width = unit_width * group

    def out_lanes(owner, unit):
        return out_hbm.at[:, lanes_of(owner, unit, out_width)]

    def out_own(unit):
        return pltpu.make_async_copy(
            stage.at[unit, core], out_lanes(core, unit), out_sem.at[unit]
        )

    def out_swap(unit):
        return send(
            stage.at[unit, 1 - core], out_lanes(core, unit),
            out_send.at[unit], out_recv.at[unit], {"head": sibling},
        )

    def finish(unit):
        for n in range(unit_heads):
            j = unit * unit_heads + n
            for g in range(group):
                head = j * group + g
                part = slice(g * chip_rows, (g + 1) * chip_rows)
                row = head % heads_dev
                gate = gate_in[core * (peers // CORES) + head // heads_dev, row : row + 1, :]
                ratio = acc[j, part, :HD] / acc[j, part, HD:]
                done = jnp.where(live, ratio * gate, jnp.float32(0.0)).astype(stage.dtype)
                at = slice((n * group + g) * HD, (n * group + g + 1) * HD)
                stage[unit, :, :, at] = done.reshape(CORES, rows, HD)
        out_swap(unit).start()
        out_own(unit).start()

    def one_level(s, carry):
        level = z - s
        for u in range(units):
            @pl.when(s < z)
            def _():
                wait_slot(level - 1, u, chip)
                issue(level - 1, u)

            @pl.when(s == 0)
            def _():
                wait_sibling(u)

            for step in range(1, chips):
                wait_slot(level, u, (chip + step) % chips)
            if by_span(u):
                @pl.when((s == z) & (z < levels - 1))
                def _():
                    for step in range(1, chips):
                        up_other(u, step).start()
            fold(level, u)

            @pl.when(s == z)
            def _():
                finish(u)
        return carry

    lax.fori_loop(0, z + 1, one_level, 0)

    for u in range(max(units - FLIGHT, 0), units):
        first_hop(u, lambda one: one.wait_send())

    def drain(s, carry):
        level = z - s
        for u in range(units):
            @pl.when(z < levels - 1)
            def _():
                up(level, u).wait_send()

            @pl.when(goes_across(level, u))
            def _():
                for step in range(1, chips):
                    across(level, u, step).wait_send()
        return carry

    lax.fori_loop(1, z + 1, drain, 0)
    for u in range(units):
        if by_span(u):
            @pl.when(z < levels - 1)
            def _():
                for step in range(1, chips):
                    up_other(u, step).wait_send()
    swap.wait_send()
    for step in range(1, peers):
        gate_copy(step).wait_send()
    for u in range(units):
        out_own(u).wait()
        out_swap(u).wait_send()
        send(
            stage.at[u, 1 - core], out_lanes(1 - core, u),
            out_send.at[u], out_recv.at[u], {"head": sibling},
        ).wait_recv()


def body(levels, peers, q, k, v, frames, noise, mask, gate):
    rows, kv_width = k.shape
    kv_heads = kv_width // HD // CORES
    group_rows = q.shape[1] // kv_width * rows * CORES
    chips = peers // CORES
    units = kv_heads
    level_spans = peers * rows // CT
    gate_rows = -(-(gate.shape[1] // HD) // 8) * 8
    hbm = pl.BlockSpec(memory_space=pltpu.HBM)
    pairs = q.shape[0] * q.shape[1] // HD * levels * peers * rows
    unit_width = kv_width // CORES // units
    out_width = q.shape[1] // CORES // units
    return pl.pallas_call(
        functools.partial(kernel, levels, peers, units),
        out_shape=jax.ShapeDtypeStruct(q.shape, q.dtype),
        in_specs=[hbm] * 7,
        out_specs=pl.BlockSpec(memory_space=pltpu.VMEM),
        scratch_shapes=[
            pltpu.VMEM((levels, units, chips, 2, CORES, rows, unit_width), k.dtype),
            pltpu.VMEM((CORES, rows, q.shape[1] // CORES), q.dtype),
            pltpu.VMEM((units, CORES, rows, out_width), q.dtype),
            pltpu.VMEM(gate.shape, gate.dtype),
            pltpu.SMEM(frames.shape, frames.dtype),
            pltpu.SMEM(noise.shape, noise.dtype),
            pltpu.SMEM(mask.shape, mask.dtype),
            pltpu.VMEM((kv_heads, group_rows, 2 * HD), jnp.float32),
            pltpu.VMEM((kv_heads, group_rows, HD), jnp.float32),
            pltpu.VMEM((level_spans, gate_rows, HD), jnp.float32),
            pltpu.VMEM((peers, gate_rows, HD), jnp.float32),
            pltpu.SemaphoreType.DMA((levels, units, chips)),
            pltpu.SemaphoreType.DMA((units, 2, 2, chips + 1)),
            pltpu.SemaphoreType.DMA((levels, units)),
            pltpu.SemaphoreType.DMA((levels, units, max(chips - 1, 1))),
            pltpu.SemaphoreType.DMA((units, max(chips - 1, 1))),
            pltpu.SemaphoreType.DMA((peers,)),
            pltpu.SemaphoreType.DMA((peers,)),
            pltpu.SemaphoreType.DMA((units, 2)),
            pltpu.SemaphoreType.DMA((5,)),
            pltpu.SemaphoreType.DMA((1,)),
            pltpu.SemaphoreType.DMA((1,)),
            pltpu.SemaphoreType.DMA((units,)),
            pltpu.SemaphoreType.DMA((units,)),
            pltpu.SemaphoreType.DMA((units,)),
        ],
        compiler_params=pltpu.CompilerParams(
            collective_id=0, has_side_effects=True, vmem_limit_bytes=48 << 20
        ),
        cost_estimate=pl.CostEstimate(
            flops=pairs * HD * 4, bytes_accessed=4 * q.size, transcendentals=pairs
        ),
    )(*[pltpu.with_memory_space_constraint(x, pltpu.HBM) for x in (q, k, v, frames, noise, mask, gate)])


def solution(mesh):
    placed = (
        P(("groups", "span", "head"), None),
        P(("groups", "span", "head"), None),
        P(("groups", "span", "head"), None),
        P("groups"),
        P("groups"),
        P("groups", None),
        P(None, "head"),
    )
    return jax.shard_map(
        functools.partial(body, mesh.shape["span"], mesh.shape["head"]),
        mesh=mesh,
        in_specs=placed,
        out_specs=P(("groups", "span", "head"), None),
        check_vma=False,
    )
```

```python
import functools
import math

import jax
import jax.numpy as jnp
from jax import lax
from jax.experimental import pallas as pl
from jax.experimental.pallas import tpu as pltpu
from jax.sharding import PartitionSpec as P

HD = 128
FRAME_TOK = 32
CT = 128
CORES = 2
FLIGHT = 2
MESH = pl.DeviceIdType.MESH
LOW = -1e30


def kernel(
    levels, peers, units,
    q_hbm, k_hbm, v_hbm, frames_hbm, noise_hbm, mask_hbm, gate_hbm,
    out_hbm,
    kv_buf, q_ref, stage, gate_ref, frames_ref, noise_ref, mask_ref, acc, top, gate_out, gate_in,
    recv_sem, first_sem, up_sem, across_sem, other_sem, gate_send, gate_recv, own_sem, load_sem,
    q_send, q_recv, out_send, out_recv, out_sem,
):
    rows, kv_width = k_hbm.shape
    kv_heads = kv_width // HD // CORES
    heads = q_hbm.shape[1] // HD // CORES
    group = heads // kv_heads
    heads_dev = gate_hbm.shape[1] // HD
    chips = peers // CORES
    chip_rows = CORES * rows
    level_rows = peers * rows
    level_spans = level_rows // CT
    unit_heads = kv_heads // units
    unit_width = unit_heads * HD
    factor = math.log2(math.e) / math.sqrt(HD)

    z = lax.axis_index("span")
    me = lax.axis_index("head")
    chip, core = me // CORES, me % CORES
    sibling = chip * CORES + (1 - core)

    barrier = pltpu.get_barrier_semaphore()
    for step in range(1, peers):
        pl.semaphore_signal(
            barrier, inc=1, device_id={"head": (me + step) % peers}, device_id_type=MESH
        )

    @pl.when(z > 0)
    def _():
        for other in (me, sibling):
            pl.semaphore_signal(
                barrier, inc=1, device_id={"span": z - 1, "head": other}, device_id_type=MESH
            )

    def lanes_of(owner, unit, width):
        start = (owner * units + unit) * width
        return pl.ds(pl.multiple_of(start, width), width)

    def piece(kv, owner, unit):
        return (k_hbm, v_hbm)[kv].at[:, lanes_of(owner, unit, unit_width)]

    def place(level, unit, slot, kv):
        return kv_buf.at[level, unit, slot, kv, core]

    def half(ref, owner):
        return ref.at[:, pl.ds(pl.multiple_of(owner * heads * HD, heads * HD), heads * HD)]

    loads = [
        pltpu.make_async_copy(source, target, load_sem.at[n])
        for n, (source, target) in enumerate(
            (
                (frames_hbm, frames_ref),
                (noise_hbm, noise_ref),
                (mask_hbm, mask_ref),
                (gate_hbm, gate_ref),
                (half(q_hbm, core), q_ref.at[core]),
            )
        )
    ]
    for load in loads:
        load.start()
    own = [
        pltpu.make_async_copy(piece(kv, core, u), place(z, u, chip, kv), own_sem.at[u, kv])
        for u in range(units)
        for kv in range(2)
    ]
    for load in own:
        load.start()

    pl.semaphore_wait(barrier, peers - 1 + jnp.where(z < levels - 1, CORES, 0))

    def send(source, target, send_sem, arrive_sem, device):
        return pltpu.make_async_remote_copy(
            src_ref=source,
            dst_ref=target,
            send_sem=send_sem,
            recv_sem=arrive_sem,
            device_id=device,
            device_id_type=MESH,
        )

    def first(unit, kv, turn, hop):
        owner = core if turn == 0 else 1 - core
        target = place(z, unit, chip, kv)
        if hop == "up":
            device = {"span": z + 1, "head": chip * CORES + owner}
            index = 0
        else:
            device = {"head": ((chip + hop) % chips) * CORES + owner}
            index = 1 + hop
        return send(
            piece(kv, owner, unit), target, first_sem.at[unit, kv, turn, index],
            recv_sem.at[z, unit, chip], device,
        )

    def first_copies(unit, turn):
        hops = list(range(1, chips)) + ([0] if turn else [])
        return [first(unit, kv, turn, hop) for hop in hops for kv in range(2)]

    def first_up(unit, turn):
        return [first(unit, kv, turn, "up") for kv in range(2)]

    def up(level, unit):
        slot = kv_buf.at[level, unit, chip]
        return send(
            slot, slot, up_sem.at[level, unit], recv_sem.at[level, unit, chip], {"span": z + 1}
        )

    def across(level, unit, step):
        slot = kv_buf.at[level, unit, chip]
        return send(
            slot, slot, across_sem.at[level, unit, step - 1], recv_sem.at[level, unit, chip],
            {"head": ((chip + step) % chips) * CORES + core},
        )

    def wait_slot(level, unit, slot):
        whole = kv_buf.at[level, unit, slot]
        send(
            whole, whole, up_sem.at[level, unit], recv_sem.at[level, unit, slot],
            {"head": sibling},
        ).wait_recv()

    def wait_sibling(unit):
        rest = kv_buf.at[z, unit, chip, :, 1 - core]
        send(
            rest, rest, up_sem.at[z, unit], recv_sem.at[z, unit, chip], {"head": sibling}
        ).wait_recv()

    def by_span(unit):
        return chips == 2 and unit % 2 == 1

    def up_other(unit, step):
        slot = kv_buf.at[0, unit, (chip + step) % chips]
        return send(
            slot, slot, other_sem.at[unit, step - 1],
            recv_sem.at[0, unit, (chip + step) % chips], {"span": z + 1},
        )

    def goes_across(level, unit):
        return (level > 0) if by_span(unit) else (level >= 0)

    def issue(level, unit):
        @pl.when(z < levels - 1)
        def _():
            up(level, unit).start()

        @pl.when(goes_across(level, unit))
        def _():
            for step in range(1, chips):
                across(level, unit, step).start()

    swap = send(
        half(q_hbm, 1 - core), q_ref.at[core], q_send.at[0], q_recv.at[0], {"head": sibling}
    )

    def gate_copy(step):
        target = (me + step) % peers
        return send(
            gate_out.at[(target * rows) // CT], gate_in.at[me],
            gate_send.at[step], gate_recv.at[me], {"head": target},
        )

    def first_hop(unit, action):
        for turn in range(2):
            @pl.when(z < levels - 1)
            def _():
                for one in first_up(unit, turn):
                    action(one)

            for one in first_copies(unit, turn):
                action(one)

    for u in range(min(FLIGHT, units)):
        first_hop(u, lambda one: one.start())
    swap.start()

    acc[...] = jnp.zeros_like(acc)
    top[...] = jnp.full_like(top, LOW)
    for load in loads:
        load.wait()
    for i in range(level_spans):
        level_index = noise_ref[z * level_spans + i]
        pick = lax.broadcasted_iota(jnp.int32, (8, gate_ref.shape[0]), 1) == level_index
        picked = jnp.dot(
            pick.astype(jnp.bfloat16), gate_ref[...], preferred_element_type=jnp.float32
        )
        for n in range(heads_dev):
            gate_out[i, n : n + 1, :] = picked[0:1, n * HD : (n + 1) * HD]
    for step in range(1, peers):
        gate_copy(step).start()

    token = chip * chip_rows
    span = z * level_spans + token // CT
    gate_in[me] = gate_out[token // CT]
    for u in range(FLIGHT, units):
        first_hop(u - FLIGHT, lambda one: one.wait_send())
        first_hop(u, lambda one: one.start())
    for load in own:
        load.wait()
    send(
        q_ref.at[1 - core], q_ref.at[1 - core], q_send.at[0], q_recv.at[0], {"head": sibling}
    ).wait_recv()
    for step in range(1, peers):
        source = (me + step) % peers
        send(
            gate_out.at[0], gate_in.at[source], gate_send.at[step], gate_recv.at[source],
            {"head": source},
        ).wait_recv()

    def fold(level, unit):
        column = lax.broadcasted_iota(jnp.int32, (1, level_rows), 1)
        usable = column < 0
        for i in range(level_spans):
            key_span = level * level_spans + i
            limit = jnp.where(mask_ref[span, key_span] > 0, frames_ref[key_span] * FRAME_TOK, 0)
            usable = usable | ((column >= i * CT) & (column < i * CT + limit))
        bias = jnp.where(usable, jnp.float32(0.0), jnp.float32(LOW))
        ones = jnp.ones((level_rows, HD), jnp.bfloat16)

        for n in range(unit_heads):
            j = unit * unit_heads + n
            lanes = slice(n * HD, (n + 1) * HD)
            queries = jnp.concatenate(
                [
                    q_ref[:, :, (j * group + g) * HD : (j * group + g + 1) * HD].reshape(
                        chip_rows, HD
                    )
                    for g in range(group)
                ],
                axis=0,
            )
            keys = kv_buf[level, unit, :, 0, :, :, lanes].reshape(level_rows, HD)
            values = kv_buf[level, unit, :, 1, :, :, lanes].reshape(level_rows, HD)
            scores = lax.dot_general(
                queries, keys, (((1,), (1,)), ((), ())), preferred_element_type=jnp.float32
            )
            scores = scores + bias
            old = top[j]
            new = jnp.maximum(old, jnp.max(scores, axis=1, keepdims=True))
            top[j] = new
            wide = jnp.concatenate([new] * (level_rows // HD), axis=1)
            weights = jnp.exp2((scores - wide) * factor).astype(jnp.bfloat16)
            update = jnp.dot(
                weights,
                jnp.concatenate([values, ones], axis=1),
                preferred_element_type=jnp.float32,
            )
            shrink = jnp.exp2((old - new) * factor)
            acc[j] = acc[j] * jnp.concatenate([shrink, shrink], axis=1) + update

    position = token % CT + lax.broadcasted_iota(jnp.int32, (chip_rows, HD), 0)
    live = position < frames_ref[span] * FRAME_TOK
    out_width = unit_width * group

    def out_lanes(owner, unit):
        return out_hbm.at[:, lanes_of(owner, unit, out_width)]

    def out_own(unit):
        return pltpu.make_async_copy(
            stage.at[unit, core], out_lanes(core, unit), out_sem.at[unit]
        )

    def out_swap(unit):
        return send(
            stage.at[unit, 1 - core], out_lanes(core, unit),
            out_send.at[unit], out_recv.at[unit], {"head": sibling},
        )

    def finish(unit):
        for n in range(unit_heads):
            j = unit * unit_heads + n
            for g in range(group):
                head = j * group + g
                part = slice(g * chip_rows, (g + 1) * chip_rows)
                row = head % heads_dev
                gate = gate_in[core * (peers // CORES) + head // heads_dev, row : row + 1, :]
                ratio = acc[j, part, :HD] / acc[j, part, HD:]
                done = jnp.where(live, ratio * gate, jnp.float32(0.0)).astype(stage.dtype)
                at = slice((n * group + g) * HD, (n * group + g + 1) * HD)
                stage[unit, :, :, at] = done.reshape(CORES, rows, HD)
        out_swap(unit).start()
        out_own(unit).start()

    def one_level(s, carry):
        level = z - s
        for u in range(units):
            ahead, ahead_unit = 1 + (u + 1) // units, (u + 1) % units

            @pl.when(s + ahead <= z)
            def _():
                wait_slot(level - ahead, ahead_unit, chip)
                issue(level - ahead, ahead_unit)

            @pl.when(s == 0)
            def _():
                wait_sibling(u)

            for step in range(1, chips):
                wait_slot(level, u, (chip + step) % chips)
            if by_span(u):
                @pl.when((s == z) & (z < levels - 1))
                def _():
                    for step in range(1, chips):
                        up_other(u, step).start()
            fold(level, u)

            @pl.when(s == z)
            def _():
                finish(u)
        return carry

    @pl.when(z > 0)
    def _():
        wait_slot(z - 1, 0, chip)
        issue(z - 1, 0)

    lax.fori_loop(0, z + 1, one_level, 0)

    for u in range(max(units - FLIGHT, 0), units):
        first_hop(u, lambda one: one.wait_send())

    def drain(s, carry):
        level = z - s
        for u in range(units):
            @pl.when(z < levels - 1)
            def _():
                up(level, u).wait_send()

            @pl.when(goes_across(level, u))
            def _():
                for step in range(1, chips):
                    across(level, u, step).wait_send()
        return carry

    lax.fori_loop(1, z + 1, drain, 0)
    for u in range(units):
        if by_span(u):
            @pl.when(z < levels - 1)
            def _():
                for step in range(1, chips):
                    up_other(u, step).wait_send()
    swap.wait_send()
    for step in range(1, peers):
        gate_copy(step).wait_send()
    for u in range(units):
        out_own(u).wait()
        out_swap(u).wait_send()
        send(
            stage.at[u, 1 - core], out_lanes(1 - core, u),
            out_send.at[u], out_recv.at[u], {"head": sibling},
        ).wait_recv()


def body(levels, peers, q, k, v, frames, noise, mask, gate):
    rows, kv_width = k.shape
    kv_heads = kv_width // HD // CORES
    group_rows = q.shape[1] // kv_width * rows * CORES
    chips = peers // CORES
    units = kv_heads
    level_spans = peers * rows // CT
    gate_rows = -(-(gate.shape[1] // HD) // 8) * 8
    hbm = pl.BlockSpec(memory_space=pltpu.HBM)
    pairs = q.shape[0] * q.shape[1] // HD * levels * peers * rows
    unit_width = kv_width // CORES // units
    out_width = q.shape[1] // CORES // units
    return pl.pallas_call(
        functools.partial(kernel, levels, peers, units),
        out_shape=jax.ShapeDtypeStruct(q.shape, q.dtype),
        in_specs=[hbm] * 7,
        out_specs=pl.BlockSpec(memory_space=pltpu.VMEM),
        scratch_shapes=[
            pltpu.VMEM((levels, units, chips, 2, CORES, rows, unit_width), k.dtype),
            pltpu.VMEM((CORES, rows, q.shape[1] // CORES), q.dtype),
            pltpu.VMEM((units, CORES, rows, out_width), q.dtype),
            pltpu.VMEM(gate.shape, gate.dtype),
            pltpu.SMEM(frames.shape, frames.dtype),
            pltpu.SMEM(noise.shape, noise.dtype),
            pltpu.SMEM(mask.shape, mask.dtype),
            pltpu.VMEM((kv_heads, group_rows, 2 * HD), jnp.float32),
            pltpu.VMEM((kv_heads, group_rows, HD), jnp.float32),
            pltpu.VMEM((level_spans, gate_rows, HD), jnp.float32),
            pltpu.VMEM((peers, gate_rows, HD), jnp.float32),
            pltpu.SemaphoreType.DMA((levels, units, chips)),
            pltpu.SemaphoreType.DMA((units, 2, 2, chips + 1)),
            pltpu.SemaphoreType.DMA((levels, units)),
            pltpu.SemaphoreType.DMA((levels, units, max(chips - 1, 1))),
            pltpu.SemaphoreType.DMA((units, max(chips - 1, 1))),
            pltpu.SemaphoreType.DMA((peers,)),
            pltpu.SemaphoreType.DMA((peers,)),
            pltpu.SemaphoreType.DMA((units, 2)),
            pltpu.SemaphoreType.DMA((5,)),
            pltpu.SemaphoreType.DMA((1,)),
            pltpu.SemaphoreType.DMA((1,)),
            pltpu.SemaphoreType.DMA((units,)),
            pltpu.SemaphoreType.DMA((units,)),
            pltpu.SemaphoreType.DMA((units,)),
        ],
        compiler_params=pltpu.CompilerParams(
            collective_id=0, has_side_effects=True, vmem_limit_bytes=48 << 20
        ),
        cost_estimate=pl.CostEstimate(
            flops=pairs * HD * 4, bytes_accessed=4 * q.size, transcendentals=pairs
        ),
    )(*[pltpu.with_memory_space_constraint(x, pltpu.HBM) for x in (q, k, v, frames, noise, mask, gate)])


def solution(mesh):
    placed = (
        P(("groups", "span", "head"), None),
        P(("groups", "span", "head"), None),
        P(("groups", "span", "head"), None),
        P("groups"),
        P("groups"),
        P("groups", None),
        P(None, "head"),
    )
    return jax.shard_map(
        functools.partial(body, mesh.shape["span"], mesh.shape["head"]),
        mesh=mesh,
        in_specs=placed,
        out_specs=P(("groups", "span", "head"), None),
        check_vma=False,
    )
```

```python
import functools
import math

import jax
import jax.numpy as jnp
from jax import lax
from jax.experimental import pallas as pl
from jax.experimental.pallas import tpu as pltpu
from jax.sharding import PartitionSpec as P

HD = 128
FRAME_TOK = 32
CT = 128
CORES = 2
FLIGHT = 2
MESH = pl.DeviceIdType.MESH
LOW = -1e30


def kernel(
    levels, peers, units,
    q_hbm, k_hbm, v_hbm, frames_hbm, noise_hbm, mask_hbm, gate_hbm,
    out_hbm,
    kv_buf, q_ref, stage, gate_ref, frames_ref, noise_ref, mask_ref, acc, top, gate_out, gate_in,
    recv_sem, first_sem, up_sem, across_sem, other_sem, gate_send, gate_recv, own_sem, load_sem,
    q_send, q_recv, out_send, out_recv, out_sem,
):
    rows, kv_width = k_hbm.shape
    kv_heads = kv_width // HD // CORES
    heads = q_hbm.shape[1] // HD // CORES
    group = heads // kv_heads
    heads_dev = gate_hbm.shape[1] // HD
    chips = peers // CORES
    chip_rows = CORES * rows
    level_rows = peers * rows
    level_spans = level_rows // CT
    unit_heads = kv_heads // units
    unit_width = unit_heads * HD
    factor = math.log2(math.e) / math.sqrt(HD)

    z = lax.axis_index("span")
    me = lax.axis_index("head")
    chip, core = me // CORES, me % CORES
    sibling = chip * CORES + (1 - core)

    barrier = pltpu.get_barrier_semaphore()
    for step in range(1, peers):
        pl.semaphore_signal(
            barrier, inc=1, device_id={"head": (me + step) % peers}, device_id_type=MESH
        )

    @pl.when(z > 0)
    def _():
        for other in (me, sibling):
            pl.semaphore_signal(
                barrier, inc=1, device_id={"span": z - 1, "head": other}, device_id_type=MESH
            )

    def lanes_of(owner, unit, width):
        start = (owner * units + unit) * width
        return pl.ds(pl.multiple_of(start, width), width)

    def piece(kv, owner, unit):
        return (k_hbm, v_hbm)[kv].at[:, lanes_of(owner, unit, unit_width)]

    def place(level, unit, slot, kv):
        return kv_buf.at[level, unit, slot, kv, core]

    def half(ref, owner):
        return ref.at[:, pl.ds(pl.multiple_of(owner * heads * HD, heads * HD), heads * HD)]

    loads = [
        pltpu.make_async_copy(source, target, load_sem.at[n])
        for n, (source, target) in enumerate(
            (
                (frames_hbm, frames_ref),
                (noise_hbm, noise_ref),
                (mask_hbm, mask_ref),
                (gate_hbm, gate_ref),
                (half(q_hbm, core), q_ref.at[core]),
            )
        )
    ]
    for load in loads:
        load.start()
    own = [
        pltpu.make_async_copy(piece(kv, core, u), place(z, u, chip, kv), own_sem.at[u, kv])
        for u in range(units)
        for kv in range(2)
    ]
    for load in own:
        load.start()

    pl.semaphore_wait(barrier, peers - 1 + jnp.where(z < levels - 1, CORES, 0))

    def send(source, target, send_sem, arrive_sem, device):
        return pltpu.make_async_remote_copy(
            src_ref=source,
            dst_ref=target,
            send_sem=send_sem,
            recv_sem=arrive_sem,
            device_id=device,
            device_id_type=MESH,
        )

    def first(unit, kv, turn, hop):
        owner = core if turn == 0 else 1 - core
        target = place(z, unit, chip, kv)
        if hop == "up":
            device = {"span": z + 1, "head": chip * CORES + owner}
            index = 0
        else:
            device = {"head": ((chip + hop) % chips) * CORES + owner}
            index = 1 + hop
        return send(
            piece(kv, owner, unit), target, first_sem.at[unit, kv, turn, index],
            recv_sem.at[z, unit, chip], device,
        )

    def first_copies(unit, turn):
        hops = list(range(1, chips)) + ([0] if turn else [])
        return [first(unit, kv, turn, hop) for hop in hops for kv in range(2)]

    def first_up(unit, turn):
        return [first(unit, kv, turn, "up") for kv in range(2)]

    def up(level, unit):
        slot = kv_buf.at[level, unit, chip]
        return send(
            slot, slot, up_sem.at[level, unit], recv_sem.at[level, unit, chip], {"span": z + 1}
        )

    def across(level, unit, step):
        slot = kv_buf.at[level, unit, chip]
        return send(
            slot, slot, across_sem.at[level, unit, step - 1], recv_sem.at[level, unit, chip],
            {"head": ((chip + step) % chips) * CORES + core},
        )

    def wait_slot(level, unit, slot):
        whole = kv_buf.at[level, unit, slot]
        send(
            whole, whole, up_sem.at[level, unit], recv_sem.at[level, unit, slot],
            {"head": sibling},
        ).wait_recv()

    def wait_sibling(unit):
        rest = kv_buf.at[z, unit, chip, :, 1 - core]
        send(
            rest, rest, up_sem.at[z, unit], recv_sem.at[z, unit, chip], {"head": sibling}
        ).wait_recv()

    def by_span(unit):
        return chips == 2 and unit % 2 == 1

    def up_other(unit, step):
        slot = kv_buf.at[0, unit, (chip + step) % chips]
        return send(
            slot, slot, other_sem.at[unit, step - 1],
            recv_sem.at[0, unit, (chip + step) % chips], {"span": z + 1},
        )

    def goes_across(level, unit):
        return (level > 0) if by_span(unit) else (level >= 0)

    def issue(level, unit):
        @pl.when(z < levels - 1)
        def _():
            up(level, unit).start()

    def start_across(level, unit):
        for step in range(1, chips):
            across(level, unit, step).start()

    swap = send(
        half(q_hbm, 1 - core), q_ref.at[core], q_send.at[0], q_recv.at[0], {"head": sibling}
    )

    def gate_copy(step):
        target = (me + step) % peers
        return send(
            gate_out.at[(target * rows) // CT], gate_in.at[me],
            gate_send.at[step], gate_recv.at[me], {"head": target},
        )

    def first_hop(unit, action):
        for turn in range(2):
            @pl.when(z < levels - 1)
            def _():
                for one in first_up(unit, turn):
                    action(one)

            for one in first_copies(unit, turn):
                action(one)

    for u in range(min(FLIGHT, units)):
        first_hop(u, lambda one: one.start())
    swap.start()

    acc[...] = jnp.zeros_like(acc)
    top[...] = jnp.full_like(top, LOW)
    for load in loads:
        load.wait()
    for i in range(level_spans):
        level_index = noise_ref[z * level_spans + i]
        pick = lax.broadcasted_iota(jnp.int32, (8, gate_ref.shape[0]), 1) == level_index
        picked = jnp.dot(
            pick.astype(jnp.bfloat16), gate_ref[...], preferred_element_type=jnp.float32
        )
        for n in range(heads_dev):
            gate_out[i, n : n + 1, :] = picked[0:1, n * HD : (n + 1) * HD]
    for step in range(1, peers):
        gate_copy(step).start()

    token = chip * chip_rows
    span = z * level_spans + token // CT
    gate_in[me] = gate_out[token // CT]
    for u in range(FLIGHT, units):
        first_hop(u - FLIGHT, lambda one: one.wait_send())
        first_hop(u, lambda one: one.start())
    for load in own:
        load.wait()
    send(
        q_ref.at[1 - core], q_ref.at[1 - core], q_send.at[0], q_recv.at[0], {"head": sibling}
    ).wait_recv()
    for step in range(1, peers):
        source = (me + step) % peers
        send(
            gate_out.at[0], gate_in.at[source], gate_send.at[step], gate_recv.at[source],
            {"head": source},
        ).wait_recv()

    def fold(level, unit):
        column = lax.broadcasted_iota(jnp.int32, (1, level_rows), 1)
        usable = column < 0
        for i in range(level_spans):
            key_span = level * level_spans + i
            limit = jnp.where(mask_ref[span, key_span] > 0, frames_ref[key_span] * FRAME_TOK, 0)
            usable = usable | ((column >= i * CT) & (column < i * CT + limit))
        bias = jnp.where(usable, jnp.float32(0.0), jnp.float32(LOW))
        ones = jnp.ones((level_rows, HD), jnp.bfloat16)

        for n in range(unit_heads):
            j = unit * unit_heads + n
            lanes = slice(n * HD, (n + 1) * HD)
            queries = jnp.concatenate(
                [
                    q_ref[:, :, (j * group + g) * HD : (j * group + g + 1) * HD].reshape(
                        chip_rows, HD
                    )
                    for g in range(group)
                ],
                axis=0,
            )
            keys = kv_buf[level, unit, :, 0, :, :, lanes].reshape(level_rows, HD)
            values = kv_buf[level, unit, :, 1, :, :, lanes].reshape(level_rows, HD)
            scores = lax.dot_general(
                queries, keys, (((1,), (1,)), ((), ())), preferred_element_type=jnp.float32
            )
            scores = scores + bias
            old = top[j]
            new = jnp.maximum(old, jnp.max(scores, axis=1, keepdims=True))
            top[j] = new
            wide = jnp.concatenate([new] * (level_rows // HD), axis=1)
            weights = jnp.exp2((scores - wide) * factor).astype(jnp.bfloat16)
            update = jnp.dot(
                weights,
                jnp.concatenate([values, ones], axis=1),
                preferred_element_type=jnp.float32,
            )
            shrink = jnp.exp2((old - new) * factor)
            acc[j] = acc[j] * jnp.concatenate([shrink, shrink], axis=1) + update

    position = token % CT + lax.broadcasted_iota(jnp.int32, (chip_rows, HD), 0)
    live = position < frames_ref[span] * FRAME_TOK
    out_width = unit_width * group

    def out_lanes(owner, unit):
        return out_hbm.at[:, lanes_of(owner, unit, out_width)]

    def out_own(unit):
        return pltpu.make_async_copy(
            stage.at[unit, core], out_lanes(core, unit), out_sem.at[unit]
        )

    def out_swap(unit):
        return send(
            stage.at[unit, 1 - core], out_lanes(core, unit),
            out_send.at[unit], out_recv.at[unit], {"head": sibling},
        )

    def finish(unit):
        for n in range(unit_heads):
            j = unit * unit_heads + n
            for g in range(group):
                head = j * group + g
                part = slice(g * chip_rows, (g + 1) * chip_rows)
                row = head % heads_dev
                gate = gate_in[core * (peers // CORES) + head // heads_dev, row : row + 1, :]
                ratio = acc[j, part, :HD] / acc[j, part, HD:]
                done = jnp.where(live, ratio * gate, jnp.float32(0.0)).astype(stage.dtype)
                at = slice((n * group + g) * HD, (n * group + g + 1) * HD)
                stage[unit, :, :, at] = done.reshape(CORES, rows, HD)
        out_swap(unit).start()
        out_own(unit).start()

    def one_level(s, carry):
        level = z - s
        for u in range(units):
            @pl.when(s < z)
            def _():
                wait_slot(level - 1, u, chip)
                issue(level - 1, u)

            @pl.when(s == 0)
            def _():
                wait_sibling(u)

            for step in range(1, chips):
                wait_slot(level, u, (chip + step) % chips)
            if by_span(u):
                @pl.when((s == z) & (z < levels - 1))
                def _():
                    for step in range(1, chips):
                        up_other(u, step).start()
            turn, later = (u + FLIGHT) // units, (u + FLIGHT) % units

            @pl.when((s + turn >= 1) & (s + turn <= z))
            def _():
                if chips != 2:
                    start_across(level - turn, later)
                else:
                    @pl.when(level - turn > 0)
                    def _():
                        start_across(level - turn, later)

                    early = later + later % 2
                    if early < units and (later == 0 or later % 2 == 1):
                        @pl.when(level - turn == 0)
                        def _():
                            start_across(level - turn, early)
            fold(level, u)

            @pl.when(s == z)
            def _():
                finish(u)
        return carry

    lax.fori_loop(0, z + 1, one_level, 0)

    for u in range(max(units - FLIGHT, 0), units):
        first_hop(u, lambda one: one.wait_send())

    def drain(s, carry):
        level = z - s
        for u in range(units):
            @pl.when(z < levels - 1)
            def _():
                up(level, u).wait_send()

            @pl.when(goes_across(level, u))
            def _():
                for step in range(1, chips):
                    across(level, u, step).wait_send()
        return carry

    lax.fori_loop(1, z + 1, drain, 0)
    for u in range(units):
        if by_span(u):
            @pl.when(z < levels - 1)
            def _():
                for step in range(1, chips):
                    up_other(u, step).wait_send()
    swap.wait_send()
    for step in range(1, peers):
        gate_copy(step).wait_send()
    for u in range(units):
        out_own(u).wait()
        out_swap(u).wait_send()
        send(
            stage.at[u, 1 - core], out_lanes(1 - core, u),
            out_send.at[u], out_recv.at[u], {"head": sibling},
        ).wait_recv()


def body(levels, peers, q, k, v, frames, noise, mask, gate):
    rows, kv_width = k.shape
    kv_heads = kv_width // HD // CORES
    group_rows = q.shape[1] // kv_width * rows * CORES
    chips = peers // CORES
    units = kv_heads
    level_spans = peers * rows // CT
    gate_rows = -(-(gate.shape[1] // HD) // 8) * 8
    hbm = pl.BlockSpec(memory_space=pltpu.HBM)
    pairs = q.shape[0] * q.shape[1] // HD * levels * peers * rows
    unit_width = kv_width // CORES // units
    out_width = q.shape[1] // CORES // units
    return pl.pallas_call(
        functools.partial(kernel, levels, peers, units),
        out_shape=jax.ShapeDtypeStruct(q.shape, q.dtype),
        in_specs=[hbm] * 7,
        out_specs=pl.BlockSpec(memory_space=pltpu.VMEM),
        scratch_shapes=[
            pltpu.VMEM((levels, units, chips, 2, CORES, rows, unit_width), k.dtype),
            pltpu.VMEM((CORES, rows, q.shape[1] // CORES), q.dtype),
            pltpu.VMEM((units, CORES, rows, out_width), q.dtype),
            pltpu.VMEM(gate.shape, gate.dtype),
            pltpu.SMEM(frames.shape, frames.dtype),
            pltpu.SMEM(noise.shape, noise.dtype),
            pltpu.SMEM(mask.shape, mask.dtype),
            pltpu.VMEM((kv_heads, group_rows, 2 * HD), jnp.float32),
            pltpu.VMEM((kv_heads, group_rows, HD), jnp.float32),
            pltpu.VMEM((level_spans, gate_rows, HD), jnp.float32),
            pltpu.VMEM((peers, gate_rows, HD), jnp.float32),
            pltpu.SemaphoreType.DMA((levels, units, chips)),
            pltpu.SemaphoreType.DMA((units, 2, 2, chips + 1)),
            pltpu.SemaphoreType.DMA((levels, units)),
            pltpu.SemaphoreType.DMA((levels, units, max(chips - 1, 1))),
            pltpu.SemaphoreType.DMA((units, max(chips - 1, 1))),
            pltpu.SemaphoreType.DMA((peers,)),
            pltpu.SemaphoreType.DMA((peers,)),
            pltpu.SemaphoreType.DMA((units, 2)),
            pltpu.SemaphoreType.DMA((5,)),
            pltpu.SemaphoreType.DMA((1,)),
            pltpu.SemaphoreType.DMA((1,)),
            pltpu.SemaphoreType.DMA((units,)),
            pltpu.SemaphoreType.DMA((units,)),
            pltpu.SemaphoreType.DMA((units,)),
        ],
        compiler_params=pltpu.CompilerParams(
            collective_id=0, has_side_effects=True, vmem_limit_bytes=48 << 20
        ),
        cost_estimate=pl.CostEstimate(
            flops=pairs * HD * 4, bytes_accessed=4 * q.size, transcendentals=pairs
        ),
    )(*[pltpu.with_memory_space_constraint(x, pltpu.HBM) for x in (q, k, v, frames, noise, mask, gate)])


def solution(mesh):
    placed = (
        P(("groups", "span", "head"), None),
        P(("groups", "span", "head"), None),
        P(("groups", "span", "head"), None),
        P("groups"),
        P("groups"),
        P("groups", None),
        P(None, "head"),
    )
    return jax.shard_map(
        functools.partial(body, mesh.shape["span"], mesh.shape["head"]),
        mesh=mesh,
        in_specs=placed,
        out_specs=P(("groups", "span", "head"), None),
        check_vma=False,
    )
```

```python
import functools
import math

import jax
import jax.numpy as jnp
from jax import lax
from jax.experimental import pallas as pl
from jax.experimental.pallas import tpu as pltpu
from jax.sharding import PartitionSpec as P

HD = 128
FRAME_TOK = 32
CT = 128
CORES = 2
FLIGHT = 3
MESH = pl.DeviceIdType.MESH
LOW = -1e30


def kernel(
    levels, peers, units,
    q_hbm, k_hbm, v_hbm, frames_hbm, noise_hbm, mask_hbm, gate_hbm,
    out_hbm,
    kv_buf, q_ref, stage, gate_ref, frames_ref, noise_ref, mask_ref, acc, top, gate_out, gate_in,
    recv_sem, first_sem, up_sem, across_sem, other_sem, gate_send, gate_recv, own_sem, load_sem,
    q_send, q_recv, out_send, out_recv, out_sem,
):
    rows, kv_width = k_hbm.shape
    kv_heads = kv_width // HD // CORES
    heads = q_hbm.shape[1] // HD // CORES
    group = heads // kv_heads
    heads_dev = gate_hbm.shape[1] // HD
    chips = peers // CORES
    chip_rows = CORES * rows
    level_rows = peers * rows
    level_spans = level_rows // CT
    unit_heads = kv_heads // units
    unit_width = unit_heads * HD
    factor = math.log2(math.e) / math.sqrt(HD)

    z = lax.axis_index("span")
    me = lax.axis_index("head")
    chip, core = me // CORES, me % CORES
    sibling = chip * CORES + (1 - core)

    barrier = pltpu.get_barrier_semaphore()
    for step in range(1, peers):
        pl.semaphore_signal(
            barrier, inc=1, device_id={"head": (me + step) % peers}, device_id_type=MESH
        )

    @pl.when(z > 0)
    def _():
        for other in (me, sibling):
            pl.semaphore_signal(
                barrier, inc=1, device_id={"span": z - 1, "head": other}, device_id_type=MESH
            )

    def lanes_of(owner, unit, width):
        start = (owner * units + unit) * width
        return pl.ds(pl.multiple_of(start, width), width)

    def piece(kv, owner, unit):
        return (k_hbm, v_hbm)[kv].at[:, lanes_of(owner, unit, unit_width)]

    def place(level, unit, slot, kv):
        return kv_buf.at[level, unit, slot, kv, core]

    def half(ref, owner):
        return ref.at[:, pl.ds(pl.multiple_of(owner * heads * HD, heads * HD), heads * HD)]

    loads = [
        pltpu.make_async_copy(source, target, load_sem.at[n])
        for n, (source, target) in enumerate(
            (
                (frames_hbm, frames_ref),
                (noise_hbm, noise_ref),
                (mask_hbm, mask_ref),
                (gate_hbm, gate_ref),
                (half(q_hbm, core), q_ref.at[core]),
            )
        )
    ]
    for load in loads:
        load.start()
    own = [
        pltpu.make_async_copy(piece(kv, core, u), place(z, u, chip, kv), own_sem.at[u, kv])
        for u in range(units)
        for kv in range(2)
    ]
    for load in own:
        load.start()

    pl.semaphore_wait(barrier, peers - 1 + jnp.where(z < levels - 1, CORES, 0))

    def send(source, target, send_sem, arrive_sem, device):
        return pltpu.make_async_remote_copy(
            src_ref=source,
            dst_ref=target,
            send_sem=send_sem,
            recv_sem=arrive_sem,
            device_id=device,
            device_id_type=MESH,
        )

    def first(unit, kv, turn, hop):
        owner = core if turn == 0 else 1 - core
        target = place(z, unit, chip, kv)
        if hop == "up":
            device = {"span": z + 1, "head": chip * CORES + owner}
            index = 0
        else:
            device = {"head": ((chip + hop) % chips) * CORES + owner}
            index = 1 + hop
        return send(
            piece(kv, owner, unit), target, first_sem.at[unit, kv, turn, index],
            recv_sem.at[z, unit, chip], device,
        )

    def first_copies(unit, turn):
        hops = list(range(1, chips)) + ([0] if turn else [])
        return [first(unit, kv, turn, hop) for hop in hops for kv in range(2)]

    def first_up(unit, turn):
        return [first(unit, kv, turn, "up") for kv in range(2)]

    def up(level, unit):
        slot = kv_buf.at[level, unit, chip]
        return send(
            slot, slot, up_sem.at[level, unit], recv_sem.at[level, unit, chip], {"span": z + 1}
        )

    def across(level, unit, step):
        slot = kv_buf.at[level, unit, chip]
        return send(
            slot, slot, across_sem.at[level, unit, step - 1], recv_sem.at[level, unit, chip],
            {"head": ((chip + step) % chips) * CORES + core},
        )

    def wait_slot(level, unit, slot):
        whole = kv_buf.at[level, unit, slot]
        send(
            whole, whole, up_sem.at[level, unit], recv_sem.at[level, unit, slot],
            {"head": sibling},
        ).wait_recv()

    def wait_sibling(unit):
        rest = kv_buf.at[z, unit, chip, :, 1 - core]
        send(
            rest, rest, up_sem.at[z, unit], recv_sem.at[z, unit, chip], {"head": sibling}
        ).wait_recv()

    def by_span(unit):
        return chips == 2 and unit % 2 == 1

    def up_other(unit, step):
        slot = kv_buf.at[0, unit, (chip + step) % chips]
        return send(
            slot, slot, other_sem.at[unit, step - 1],
            recv_sem.at[0, unit, (chip + step) % chips], {"span": z + 1},
        )

    def goes_across(level, unit):
        return (level > 0) if by_span(unit) else (level >= 0)

    def issue(level, unit):
        @pl.when(z < levels - 1)
        def _():
            up(level, unit).start()

        @pl.when(goes_across(level, unit))
        def _():
            for step in range(1, chips):
                across(level, unit, step).start()

    swap = send(
        half(q_hbm, 1 - core), q_ref.at[core], q_send.at[0], q_recv.at[0], {"head": sibling}
    )

    def gate_copy(step):
        target = (me + step) % peers
        return send(
            gate_out.at[(target * rows) // CT], gate_in.at[me],
            gate_send.at[step], gate_recv.at[me], {"head": target},
        )

    def first_hop(unit, action):
        for turn in range(2):
            @pl.when(z < levels - 1)
            def _():
                for one in first_up(unit, turn):
                    action(one)

            for one in first_copies(unit, turn):
                action(one)

    for u in range(min(FLIGHT, units)):
        first_hop(u, lambda one: one.start())
    swap.start()

    acc[...] = jnp.zeros_like(acc)
    top[...] = jnp.full_like(top, LOW)
    for load in loads:
        load.wait()
    for i in range(level_spans):
        level_index = noise_ref[z * level_spans + i]
        pick = lax.broadcasted_iota(jnp.int32, (8, gate_ref.shape[0]), 1) == level_index
        picked = jnp.dot(
            pick.astype(jnp.bfloat16), gate_ref[...], preferred_element_type=jnp.float32
        )
        for n in range(heads_dev):
            gate_out[i, n : n + 1, :] = picked[0:1, n * HD : (n + 1) * HD]
    for step in range(1, peers):
        gate_copy(step).start()

    token = chip * chip_rows
    span = z * level_spans + token // CT
    gate_in[me] = gate_out[token // CT]
    for u in range(FLIGHT, units):
        first_hop(u - FLIGHT, lambda one: one.wait_send())
        first_hop(u, lambda one: one.start())
    for load in own:
        load.wait()
    send(
        q_ref.at[1 - core], q_ref.at[1 - core], q_send.at[0], q_recv.at[0], {"head": sibling}
    ).wait_recv()
    for step in range(1, peers):
        source = (me + step) % peers
        send(
            gate_out.at[0], gate_in.at[source], gate_send.at[step], gate_recv.at[source],
            {"head": source},
        ).wait_recv()

    def fold(level, unit):
        column = lax.broadcasted_iota(jnp.int32, (1, level_rows), 1)
        usable = column < 0
        for i in range(level_spans):
            key_span = level * level_spans + i
            limit = jnp.where(mask_ref[span, key_span] > 0, frames_ref[key_span] * FRAME_TOK, 0)
            usable = usable | ((column >= i * CT) & (column < i * CT + limit))
        bias = jnp.where(usable, jnp.float32(0.0), jnp.float32(LOW))
        ones = jnp.ones((level_rows, HD), jnp.bfloat16)

        for n in range(unit_heads):
            j = unit * unit_heads + n
            lanes = slice(n * HD, (n + 1) * HD)
            queries = jnp.concatenate(
                [
                    q_ref[:, :, (j * group + g) * HD : (j * group + g + 1) * HD].reshape(
                        chip_rows, HD
                    )
                    for g in range(group)
                ],
                axis=0,
            )
            keys = kv_buf[level, unit, :, 0, :, :, lanes].reshape(level_rows, HD)
            values = kv_buf[level, unit, :, 1, :, :, lanes].reshape(level_rows, HD)
            scores = lax.dot_general(
                queries, keys, (((1,), (1,)), ((), ())), preferred_element_type=jnp.float32
            )
            scores = scores + bias
            old = top[j]
            new = jnp.maximum(old, jnp.max(scores, axis=1, keepdims=True))
            top[j] = new
            wide = jnp.concatenate([new] * (level_rows // HD), axis=1)
            weights = jnp.exp2((scores - wide) * factor).astype(jnp.bfloat16)
            update = jnp.dot(
                weights,
                jnp.concatenate([values, ones], axis=1),
                preferred_element_type=jnp.float32,
            )
            shrink = jnp.exp2((old - new) * factor)
            acc[j] = acc[j] * jnp.concatenate([shrink, shrink], axis=1) + update

    position = token % CT + lax.broadcasted_iota(jnp.int32, (chip_rows, HD), 0)
    live = position < frames_ref[span] * FRAME_TOK
    out_width = unit_width * group

    def out_lanes(owner, unit):
        return out_hbm.at[:, lanes_of(owner, unit, out_width)]

    def out_own(unit):
        return pltpu.make_async_copy(
            stage.at[unit, core], out_lanes(core, unit), out_sem.at[unit]
        )

    def out_swap(unit):
        return send(
            stage.at[unit, 1 - core], out_lanes(core, unit),
            out_send.at[unit], out_recv.at[unit], {"head": sibling},
        )

    def finish(unit):
        for n in range(unit_heads):
            j = unit * unit_heads + n
            for g in range(group):
                head = j * group + g
                part = slice(g * chip_rows, (g + 1) * chip_rows)
                row = head % heads_dev
                gate = gate_in[core * (peers // CORES) + head // heads_dev, row : row + 1, :]
                ratio = acc[j, part, :HD] / acc[j, part, HD:]
                done = jnp.where(live, ratio * gate, jnp.float32(0.0)).astype(stage.dtype)
                at = slice((n * group + g) * HD, (n * group + g + 1) * HD)
                stage[unit, :, :, at] = done.reshape(CORES, rows, HD)
        out_swap(unit).start()
        out_own(unit).start()

    def one_level(s, carry):
        level = z - s
        for u in range(units):
            @pl.when(s < z)
            def _():
                wait_slot(level - 1, u, chip)
                issue(level - 1, u)

            @pl.when(s == 0)
            def _():
                wait_sibling(u)

            for step in range(1, chips):
                wait_slot(level, u, (chip + step) % chips)
            if by_span(u):
                @pl.when((s == z) & (z < levels - 1))
                def _():
                    for step in range(1, chips):
                        up_other(u, step).start()
            fold(level, u)

            @pl.when(s == z)
            def _():
                finish(u)
        return carry

    lax.fori_loop(0, z + 1, one_level, 0)

    for u in range(max(units - FLIGHT, 0), units):
        first_hop(u, lambda one: one.wait_send())

    def drain(s, carry):
        level = z - s
        for u in range(units):
            @pl.when(z < levels - 1)
            def _():
                up(level, u).wait_send()

            @pl.when(goes_across(level, u))
            def _():
                for step in range(1, chips):
                    across(level, u, step).wait_send()
        return carry

    lax.fori_loop(1, z + 1, drain, 0)
    for u in range(units):
        if by_span(u):
            @pl.when(z < levels - 1)
            def _():
                for step in range(1, chips):
                    up_other(u, step).wait_send()
    swap.wait_send()
    for step in range(1, peers):
        gate_copy(step).wait_send()
    for u in range(units):
        out_own(u).wait()
        out_swap(u).wait_send()
        send(
            stage.at[u, 1 - core], out_lanes(1 - core, u),
            out_send.at[u], out_recv.at[u], {"head": sibling},
        ).wait_recv()


def body(levels, peers, q, k, v, frames, noise, mask, gate):
    rows, kv_width = k.shape
    kv_heads = kv_width // HD // CORES
    group_rows = q.shape[1] // kv_width * rows * CORES
    chips = peers // CORES
    units = kv_heads
    level_spans = peers * rows // CT
    gate_rows = -(-(gate.shape[1] // HD) // 8) * 8
    hbm = pl.BlockSpec(memory_space=pltpu.HBM)
    pairs = q.shape[0] * q.shape[1] // HD * levels * peers * rows
    unit_width = kv_width // CORES // units
    out_width = q.shape[1] // CORES // units
    return pl.pallas_call(
        functools.partial(kernel, levels, peers, units),
        out_shape=jax.ShapeDtypeStruct(q.shape, q.dtype),
        in_specs=[hbm] * 7,
        out_specs=pl.BlockSpec(memory_space=pltpu.VMEM),
        scratch_shapes=[
            pltpu.VMEM((levels, units, chips, 2, CORES, rows, unit_width), k.dtype),
            pltpu.VMEM((CORES, rows, q.shape[1] // CORES), q.dtype),
            pltpu.VMEM((units, CORES, rows, out_width), q.dtype),
            pltpu.VMEM(gate.shape, gate.dtype),
            pltpu.SMEM(frames.shape, frames.dtype),
            pltpu.SMEM(noise.shape, noise.dtype),
            pltpu.SMEM(mask.shape, mask.dtype),
            pltpu.VMEM((kv_heads, group_rows, 2 * HD), jnp.float32),
            pltpu.VMEM((kv_heads, group_rows, HD), jnp.float32),
            pltpu.VMEM((level_spans, gate_rows, HD), jnp.float32),
            pltpu.VMEM((peers, gate_rows, HD), jnp.float32),
            pltpu.SemaphoreType.DMA((levels, units, chips)),
            pltpu.SemaphoreType.DMA((units, 2, 2, chips + 1)),
            pltpu.SemaphoreType.DMA((levels, units)),
            pltpu.SemaphoreType.DMA((levels, units, max(chips - 1, 1))),
            pltpu.SemaphoreType.DMA((units, max(chips - 1, 1))),
            pltpu.SemaphoreType.DMA((peers,)),
            pltpu.SemaphoreType.DMA((peers,)),
            pltpu.SemaphoreType.DMA((units, 2)),
            pltpu.SemaphoreType.DMA((5,)),
            pltpu.SemaphoreType.DMA((1,)),
            pltpu.SemaphoreType.DMA((1,)),
            pltpu.SemaphoreType.DMA((units,)),
            pltpu.SemaphoreType.DMA((units,)),
            pltpu.SemaphoreType.DMA((units,)),
        ],
        compiler_params=pltpu.CompilerParams(
            collective_id=0, has_side_effects=True, vmem_limit_bytes=48 << 20
        ),
        cost_estimate=pl.CostEstimate(
            flops=pairs * HD * 4, bytes_accessed=4 * q.size, transcendentals=pairs
        ),
    )(*[pltpu.with_memory_space_constraint(x, pltpu.HBM) for x in (q, k, v, frames, noise, mask, gate)])


def solution(mesh):
    placed = (
        P(("groups", "span", "head"), None),
        P(("groups", "span", "head"), None),
        P(("groups", "span", "head"), None),
        P("groups"),
        P("groups"),
        P("groups", None),
        P(None, "head"),
    )
    return jax.shard_map(
        functools.partial(body, mesh.shape["span"], mesh.shape["head"]),
        mesh=mesh,
        in_specs=placed,
        out_specs=P(("groups", "span", "head"), None),
        check_vma=False,
    )
```
